128 devices in a mesh: gx: 8 (over x, y_lo), gy: 4 (over y_hi, core), gz: 4 (over z).
Axes of the slice: x: 4, y: 4 (y_hi: 2, y_lo: 2; y = y_hi * 2 + y_lo), z: 4, core: 2. Of those that a mesh axis runs over, the one named last changes fastest.
Arguments:
- tokens: bfloat16 [1024, 4096], P('gy', ('gz', 'gx')), may hold values from -6 to 6
- cotangent: bfloat16 [1024, 4096], P('gy', ('gz', 'gx')), may hold values from -6 to 6
- gate_weight: bfloat16 [4096, 16384], P('gz', ('gx', 'gy')), may hold values from -0.09375 to 0.09375
- up_weight: bfloat16 [4096, 16384], P('gz', ('gx', 'gy')), may hold values from -0.09375 to 0.09375
- down_weight: bfloat16 [16384, 4096], P('gx', ('gz', 'gy')), may hold values from -0.046875 to 0.046875
Outputs:
- layer_out: bfloat16 [1024, 4096], P('gy', ('gz', 'gx'))
- grad_tokens: bfloat16 [1024, 4096], P('gy', ('gz', 'gx'))
- grad_gate: float32 [4096, 16384], P('gz', ('gx', 'gy'))
- grad_up: float32 [4096, 16384], P('gz', ('gx', 'gy'))
- grad_down: float32 [16384, 4096], P('gx', ('gz', 'gy'))
The draws below stay inside these ranges and needn't reach their ends.
All inputs are finite; a program needn't handle non-finite values.
Results may differ from the reference program's by a relative error of at most 0.0049.
Values may be sent and summed in bfloat16 or wider, within the bound.
A program may use at most 128 MiB of HBM per device.

```python
import jax
import jax.numpy as jnp

D = 4096
FF = 16384
TOKENS = 1024


def block_levels(stream_key, shape, pieces, low, high):
    gain, own = 1.0, jax.random.fold_in(stream_key, 6)
    for dim, parts in pieces:
        heights = jnp.exp(jax.random.uniform(jax.random.fold_in(own, dim), (parts,), jnp.float32, low / len(pieces), high / len(pieces)))
        gain = gain * jnp.repeat(heights, shape[dim] // parts).reshape([-1 if axis == dim else 1 for axis in range(len(shape))])
    return gain


def gaussian(key, shape, width, limit, shards=(), held_as=jnp.bfloat16):
    level = block_levels(key, shape, shards, -0.22, 0.18) if shards else 1.0
    array = jax.random.normal(key, shape, jnp.float32) * width * level
    return jnp.minimum(jnp.maximum(array, -limit), limit).astype(held_as)


def setup_inputs(seed: int = 0) -> dict:
    key_of = jax.random.split(jax.random.key(seed), 6)
    return {
        "tokens": gaussian(key_of[0], (TOKENS, D), 1.0, 6.0, ((0, 4), (1, 32))),
        "cotangent": gaussian(key_of[1], (TOKENS, D), 1.0, 6.0, ((0, 4), (1, 32))),
        "gate_weight": gaussian(key_of[2], (D, FF), D ** -0.5, 0.09375, ((0, 4), (1, 32))),
        "up_weight": gaussian(key_of[3], (D, FF), D ** -0.5, 0.09375, ((0, 4), (1, 32))),
        "down_weight": gaussian(key_of[4], (FF, D), FF ** -0.5, 0.046875, ((0, 8), (1, 16))),
    }


def reference(tokens, cotangent, gate_weight, up_weight, down_weight):
    gate = jnp.dot(tokens, gate_weight, preferred_element_type=jnp.float32)
    up = jnp.dot(tokens, up_weight, preferred_element_type=jnp.float32)
    sigma = jax.nn.sigmoid(gate)
    swish = gate * sigma
    hidden = (swish * up).astype(jnp.bfloat16)
    layer_out = jnp.dot(hidden, down_weight, preferred_element_type=jnp.float32).astype(jnp.bfloat16)
    grad_hidden = jnp.dot(cotangent, down_weight.T, preferred_element_type=jnp.float32)
    grad_pre_gate = (grad_hidden * up * sigma * (1.0 + gate * (1.0 - sigma))).astype(jnp.bfloat16)
    grad_pre_up = (grad_hidden * swish).astype(jnp.bfloat16)
    grad_tokens = (jnp.dot(grad_pre_gate, gate_weight.T, preferred_element_type=jnp.float32)
                   + jnp.dot(grad_pre_up, up_weight.T, preferred_element_type=jnp.float32)).astype(jnp.bfloat16)
    grad_gate = jnp.dot(tokens.T, grad_pre_gate, preferred_element_type=jnp.float32)
    grad_up = jnp.dot(tokens.T, grad_pre_up, preferred_element_type=jnp.float32)
    grad_down = jnp.dot(hidden.T, cotangent, preferred_element_type=jnp.float32)
    return layer_out, grad_tokens, grad_gate, grad_up, grad_down
```

```python
import jax
import jax.numpy as jnp
from jax import lax
from jax.experimental import pallas as pl
from jax.experimental.pallas import tpu as pltpu
from jax.sharding import PartitionSpec as P

MESH = pl.DeviceIdType.MESH
BF, F32 = jnp.bfloat16, jnp.float32
XT = jnp.bfloat16
YT = jnp.float32
NSEM = 160


def dot(a, b, dims):
    return lax.dot_general(a, b, (dims, ((), ())), preferred_element_type=F32)


class Net:
    def __init__(self, send, recv):
        self.send, self.recv, self.used, self.out = send, recv, 0, []

    def slot(self):
        self.used += 1
        return self.used - 1

    def push(self, src, dst, device, k=None):
        k = self.slot() if k is None else k
        copy = pltpu.make_async_remote_copy(
            src_ref=src, dst_ref=dst, send_sem=self.send.at[k], recv_sem=self.recv.at[k],
            device_id=device, device_id_type=MESH)
        copy.start()
        self.out.append(copy)
        return k

    def local(self, src, dst):
        k = self.slot()
        copy = pltpu.make_async_copy(src, dst, self.recv.at[k])
        copy.start()
        return copy

    def arrived(self, k, landing):
        pltpu.make_async_copy(landing, landing, self.recv.at[k]).wait()

    def drain(self):
        for copy in self.out:
            copy.wait_send()
        self.out = []


class ReduceScatter:
    def __init__(self, net, part, sent, half, full, pos, plus, minus):
        self.net, self.part, self.sent, self.half, self.full = net, part, sent, half, full
        self.pos, self.plus, self.minus = pos, plus, minus
        self.rows = sent.shape[1]

    def start(self):
        m = self.rows // 2
        sent, net = self.sent, self.net
        sent[0] = self.part[(self.pos + 2) % 4].astype(sent.dtype)
        self.ka = net.push(sent.at[0, pl.ds(0, m)], self.half.at[0], self.plus)
        self.kb = net.push(sent.at[0, pl.ds(m, m)], self.half.at[1], self.minus)

    def middle(self):
        m = self.rows // 2
        sent, net, half = self.sent, self.net, self.half
        right, left = (self.pos + 1) % 4, (self.pos + 3) % 4
        sent[1, m:] = self.part[right, m:].astype(sent.dtype)
        sent[2, :m] = self.part[left, :m].astype(sent.dtype)
        net.arrived(self.ka, half.at[0])
        sent[1, :m] = (self.part[right, :m] + half[0].astype(F32)).astype(sent.dtype)
        self.kp = net.push(sent.at[1], self.full.at[0], self.plus)
        net.arrived(self.kb, half.at[1])
        sent[2, m:] = (self.part[left, m:] + half[1].astype(F32)).astype(sent.dtype)
        self.km = net.push(sent.at[2], self.full.at[1], self.minus)

    def finish(self):
        self.net.arrived(self.kp, self.full.at[0])
        self.net.arrived(self.km, self.full.at[1])
        return self.part[self.pos] + self.full[0].astype(F32) + self.full[1].astype(F32)


class AllGather:
    def __init__(self, net, slots, pos, plus, minus):
        self.net, self.slots, self.pos, self.plus, self.minus = net, slots, pos, plus, minus
        self.rows = slots.shape[1]

    def start(self):
        own = self.slots.at[self.pos]
        self.kp = self.net.push(own, own, self.plus)
        self.km = self.net.push(own, own, self.minus)

    def forward(self):
        m = self.rows // 2
        right, left = (self.pos + 1) % 4, (self.pos + 3) % 4
        self.net.arrived(self.kp, self.slots.at[left])
        first = self.slots.at[left, pl.ds(0, m)]
        self.ka = self.net.push(first, first, self.plus)
        self.net.arrived(self.km, self.slots.at[right])
        second = self.slots.at[right, pl.ds(m, m)]
        self.kb = self.net.push(second, second, self.minus)

    def finish(self):
        m = self.rows // 2
        far = (self.pos + 2) % 4
        self.net.arrived(self.ka, self.slots.at[far, pl.ds(0, m)])
        self.net.arrived(self.kb, self.slots.at[far, pl.ds(m, m)])


def kernel(tok, cot, wg, wu, wd, lo, gt, t_out, g_out, gd_out,
           T, C, W, V, H, G, PG, PH, GU, sg, hg, fg, sh, hh, fh,
           own, give, take, sx, hx, fx, sy, ry, gs, gr, send, recv):
    gx, gy, gz = lax.axis_index("gx"), lax.axis_index("gy"), lax.axis_index("gz")
    x, z, c = gx // 2, gz, gy % 2
    yh, yl = gy // 2, gx % 2
    y = yh * 2 + yl

    def at(x, y, z, c):
        return (x * 2 + y % 2, (y // 2) * 2 + c, z)

    ys = [at(x, (y + d) % 4, z, c) for d in (1, 2, 3)]
    xs = [at((x + d) % 4, y, z, c) for d in (1, 2, 3)]
    zp, zm = at(x, y, (z + 1) % 4, c), at(x, y, (z + 3) % 4, c)
    mate = at(x, y, z, 1 - c)
    cross = at(x, (y + 2) % 4, z, 1 - c)
    net = Net(send, recv)

    loads = [net.local(tok, T.at[gy, :, pl.ds(pl.multiple_of(gx * 128, 128), 128)]),
             net.local(cot, C.at[gy, :, pl.ds(pl.multiple_of(gx * 128, 128), 128)])]
    w_loads = [net.local(wg, W.at[:, pl.ds(0, 512)]), net.local(wu, W.at[:, pl.ds(512, 512)])]
    v_load = net.local(wd.at[pl.ds(pl.multiple_of(gy * 512, 512), 512)],
                       V.at[:, pl.ds(pl.multiple_of(gy * 256, 256), 256)])

    barrier = pltpu.get_barrier_semaphore()
    peers = ys + xs + [zp, zm, mate, cross]
    for peer in peers:
        pl.semaphore_signal(barrier, inc=1, device_id=peer, device_id_type=MESH)
    pl.semaphore_wait(barrier, len(peers))

    def gather_y(src, buf):
        mine = buf.at[gy, :, pl.ds(pl.multiple_of(gx * 128, 128), 128)]
        ks = [net.push(src, mine, d) for d in ys]

        def done():
            for d, k in zip((3, 2, 1), ks):
                yy = (y + d) % 4
                g2, col = (yy // 2) * 2 + c, pl.multiple_of((x * 2 + yy % 2) * 128, 128)
                net.arrived(k, buf.at[g2, :, pl.ds(col, 128)])
        return done

    def gather_x(buf, h):
        g2 = h * 2 + c
        mine = buf.at[g2, :, pl.ds(pl.multiple_of(x * 256, 256), 256)]
        ks = [net.push(mine, mine, d) for d in xs]

        def done():
            for d, k in zip((3, 2, 1), ks):
                net.arrived(k, buf.at[g2, :, pl.ds(pl.multiple_of(((x + d) % 4) * 256, 256), 256)])
        return done

    def share(buf, h):
        mine = buf.at[h * 2 + c]
        k = net.push(mine, mine, mate)
        return lambda: net.arrived(k, buf.at[h * 2 + 1 - c])

    chunk = [c, 1 - c, 2 + 1 - c, 2 + c]

    rs_g = [ReduceScatter(net, PG.at[i], sg.at[i], hg.at[i], fg.at[i], z, zp, zm) for i in range(4)]
    rs_h = [ReduceScatter(net, PH.at[i], sh.at[i], hh.at[i], fh.at[i], z, zp, zm) for i in range(4)]
    ag_h = [AllGather(net, H.at[chunk[i]], z, zp, zm) for i in range(4)]
    ag_g = [AllGather(net, G.at[chunk[i]], z, zp, zm) for i in range(4)]

    def g1(i):
        def body(n, _):
            cols = pl.ds(pl.multiple_of(n * 256, 256), 256)
            PG[i, :, :, cols] = dot(T[chunk[i]], W[:, cols], ((1,), (0,))).reshape(4, 64, 256)
            return 0
        lax.fori_loop(0, 4, body, 0)
        rs_g[i].start()

    def g3(i):
        s = rs_g[i].finish()
        GU[i] = s
        gate, up = s[:, :512], s[:, 512:]
        H[chunk[i], z] = (gate * jax.nn.sigmoid(gate) * up).astype(BF)
        ag_h[i].start()

    def h1(i):
        def body(n, _):
            rows = pl.ds(pl.multiple_of(n * 256, 256), 256)
            PH[i, :, :, rows] = dot(C[chunk[i]], V[rows, :], ((1,), (1,))).reshape(4, 64, 256)
            return 0
        lax.fori_loop(0, 2, body, 0)
        rs_h[i].start()

    def h3(i):
        grad = rs_h[i].finish()
        gate, up = GU[i, :, :512], GU[i, :, 512:]
        s = jax.nn.sigmoid(gate)
        G[chunk[i], z, :, :512] = (grad * up * s * (1.0 + gate * (1.0 - s))).astype(BF)
        G[chunk[i], z, :, 512:] = (grad * (gate * s)).astype(BF)
        ag_g[i].start()

    took = {}

    def place(m, i):
        return (own.at[m, 0], give.at[m, 0], give.at[m, 1], own.at[m, 1])[i]

    def give_mate(m, i):
        if i in (1, 2):
            took[m, i - 1] = net.push(give.at[m, i - 1], take.at[m, i - 1], mate)

    def g5(i):
        ag_h[i].finish()
        dst = place(0, i)

        def body(n, _):
            cols = pl.ds(pl.multiple_of(n * 256, 256), 256)
            dst[n] = dot(H[chunk[i]].reshape(256, 512), V[:, cols], ((1,), (0,)))
            return 0
        lax.fori_loop(0, 4, body, 0)
        give_mate(0, i)

    def h5(i):
        ag_g[i].finish()
        dst = place(1, i)

        def body(n, _):
            rows = pl.ds(pl.multiple_of(n * 256, 256), 256)
            dst[n] = dot(G[chunk[i]].reshape(256, 1024), W[rows, :], ((1,), (1,)))
            return 0
        lax.fori_loop(0, 4, body, 0)
        give_mate(1, i)

    rs_x = [[ReduceScatter(net, own.at[m, o], sx.at[m, o], hx.at[m, o], fx.at[m, o], x, xs[0], xs[2])
             for o in range(2)] for m in range(2)]

    def x1(m, o):
        net.arrived(took[m, o], take.at[m, o])

        def body(n, _):
            own[m, o, n] += take[m, o, n]
            return 0
        lax.fori_loop(0, 4, body, 0)
        rs_x[m][o].start()

    ky = [[[net.slot() for _ in range(3)] for _ in range(2)] for _ in range(2)]

    def y_copy(m, o, t, d):
        k = ky[m][o][d - 1]
        return pltpu.make_async_remote_copy(
            src_ref=sy.at[m, o, t], dst_ref=ry.at[m, d - 1],
            send_sem=send.at[k], recv_sem=recv.at[k],
            device_id=at(x, 2 * o + t, z, c), device_id_type=MESH)

    def x3(m, o):
        r = rs_x[m][o].finish()
        sy[m, o, 0] = r[:, :128].astype(YT)
        sy[m, o, 1] = r[:, 128:].astype(YT)
        for t in range(2):
            for d in (1, 2, 3):
                @pl.when((y + d) % 4 == 2 * o + t)
                def _():
                    y_copy(m, o, t, d).start()

    def y_sent(m, o):
        for t in range(2):
            for d in (1, 2, 3):
                @pl.when((y + d) % 4 == 2 * o + t)
                def _():
                    y_copy(m, o, t, d).wait_send()

    def y_done(m, o, out):
        @pl.when(yh == o)
        def _():
            total = sy[m, o, yl].astype(F32)
            for d in (1, 2, 3):
                net.arrived(ky[m][o][d - 1], ry.at[m, d - 1])
                total += ry[m, d - 1].astype(F32)
            out[...] = total.astype(BF)

    gk = []

    def down_grad():
        def body(g, _):
            cols = pl.ds(pl.multiple_of(g * 256, 256), 256)
            gs[g] = dot(H[...].reshape(1024, 512), C[:, :, cols].reshape(1024, 256), ((0,), (0,))).astype(BF)
            return 0
        lax.fori_loop(0, 4, body, 0)
        g_mate, g_y, g_cross = yh * 2 + 1 - c, (1 - yh) * 2 + c, (1 - yh) * 2 + 1 - c
        gk.append((net.push(gs.at[g_y], gr.at[gy], ys[1]), g_y))
        gk.append((net.push(gs.at[g_cross], gr.at[gy], cross), g_cross))
        gk.append((net.push(gs.at[g_mate], gr.at[gy], mate), g_mate))
        gr[gy] = gs[gy]

    def down_share():
        g_mate, g_y, g_cross = yh * 2 + 1 - c, (1 - yh) * 2 + c, (1 - yh) * 2 + 1 - c
        dst = V.at[:, pl.ds(pl.multiple_of(gy * 256, 256), 256)]

        def rows(g):
            return wd.at[pl.ds(pl.multiple_of(g * 512, 512), 512)]
        ks = [(net.push(rows(g_y), dst, ys[1]), g_y), (net.push(rows(g_cross), dst, cross), g_cross),
              (net.push(rows(g_mate), dst, mate), g_mate)]

        def done():
            for k, g in ks:
                net.arrived(k, V.at[:, pl.ds(pl.multiple_of(g * 256, 256), 256)])
            v_load.wait()
        return done

    ty = gather_y(tok, T)
    for copy in loads:
        copy.wait()
    ty()
    tx = [gather_x(T, 0), gather_x(T, 1)]
    cy = gather_y(cot, C)
    vs = down_share()
    for copy in w_loads:
        copy.wait()
    tx[0]()
    t_mate = [share(T, 0)]
    g1(0)
    t_mate[0]()
    g1(1)
    rs_g[0].middle()
    tx[1]()
    t_mate.append(share(T, 1))
    cy()
    cx = [gather_x(C, 0), gather_x(C, 1)]
    t_mate[1]()
    g1(2)
    rs_g[1].middle()
    g3(0)
    g1(3)
    keep = [net.local(T, t_out)]
    rs_g[2].middle()
    g3(1)
    ag_h[0].forward()
    rs_g[3].middle()
    g3(2)
    ag_h[1].forward()
    vs()
    cx[0]()
    c_mate = [share(C, 0)]
    h1(0)
    g5(0)
    g3(3)
    ag_h[2].forward()
    c_mate[0]()
    h1(1)
    g5(1)
    rs_h[0].middle()
    ag_h[3].forward()
    cx[1]()
    c_mate.append(share(C, 1))
    x1(0, 0)
    g5(2)
    c_mate[1]()
    h1(2)
    rs_h[1].middle()
    h3(0)
    rs_x[0][0].middle()
    g5(3)
    x1(0, 1)
    h1(3)
    rs_h[2].middle()
    h3(1)
    ag_g[0].forward()
    x3(0, 0)
    down_grad()
    rs_x[0][1].middle()
    rs_h[3].middle()
    h3(2)
    ag_g[1].forward()
    h5(0)
    h3(3)
    ag_g[2].forward()
    h5(1)
    x3(0, 1)
    x1(1, 0)
    ag_g[3].forward()
    h5(2)
    rs_x[1][0].middle()
    h5(3)
    keep.append(net.local(G, g_out))
    x1(1, 1)
    rs_x[1][1].middle()
    x3(1, 0)
    for k, g in gk:
        net.arrived(k, gr.at[g])
    keep.append(net.local(gr, gd_out))
    y_done(0, 0, lo)
    y_done(0, 1, lo)
    x3(1, 1)
    y_done(1, 0, gt)
    y_done(1, 1, gt)
    for copy in keep:
        copy.wait()
    for m in range(2):
        for o in range(2):
            y_sent(m, o)
    net.drain()


def local(tok, cot, wg, wu, wd):
    any_, vmem = pl.BlockSpec(memory_space=pl.ANY), pl.BlockSpec(memory_space=pltpu.VMEM)
    S = jax.ShapeDtypeStruct
    scratch = [
        pltpu.VMEM((4, 256, 1024), BF),
        pltpu.VMEM((4, 256, 1024), BF),
        pltpu.VMEM((1024, 1024), BF),
        pltpu.VMEM((512, 1024), BF),
        pltpu.VMEM((4, 4, 64, 512), BF),
        pltpu.VMEM((4, 4, 64, 1024), BF),
        pltpu.VMEM((4, 4, 64, 1024), F32),
        pltpu.VMEM((4, 4, 64, 512), F32),
        pltpu.VMEM((4, 64, 1024), F32),
        pltpu.VMEM((4, 3, 64, 1024), BF),
        pltpu.VMEM((4, 2, 32, 1024), BF),
        pltpu.VMEM((4, 2, 64, 1024), BF),
        pltpu.VMEM((4, 3, 64, 512), BF),
        pltpu.VMEM((4, 2, 32, 512), BF),
        pltpu.VMEM((4, 2, 64, 512), BF),
        pltpu.VMEM((2, 2, 4, 256, 256), F32),
        pltpu.VMEM((2, 2, 4, 256, 256), F32),
        pltpu.VMEM((2, 2, 4, 256, 256), F32),
        pltpu.VMEM((2, 2, 3, 256, 256), XT),
        pltpu.VMEM((2, 2, 2, 128, 256), XT),
        pltpu.VMEM((2, 2, 2, 256, 256), XT),
        pltpu.VMEM((2, 2, 2, 256, 128), YT),
        pltpu.VMEM((2, 3, 256, 128), YT),
        pltpu.VMEM((4, 512, 256), BF),
        pltpu.VMEM((4, 512, 256), BF),
        pltpu.SemaphoreType.DMA((NSEM,)),
        pltpu.SemaphoreType.DMA((NSEM,)),
    ]
    lo, gt, t_all, g_all, gd = pl.pallas_call(
        kernel,
        out_shape=[S((256, 128), BF), S((256, 128), BF), S((4, 256, 1024), BF),
                   S((4, 4, 64, 1024), BF), S((4, 512, 256), BF)],
        in_specs=[any_] * 5,
        out_specs=[vmem, vmem, any_, any_, any_],
        scratch_shapes=scratch,
        compiler_params=pltpu.CompilerParams(
            collective_id=0, has_side_effects=True, vmem_limit_bytes=56 << 20),
        cost_estimate=pl.CostEstimate(flops=8_000_000_000, bytes_accessed=10_000_000, transcendentals=600_000),
        name="layer",
    )(tok, cot, wg, wu, wd)
    t_all = t_all.reshape(1024, 1024)
    g_all = g_all.reshape(1024, 1024)
    tn = ((0,), (0,))
    grad_gate = dot(t_all, g_all[:, :512], tn)
    grad_up = dot(t_all, g_all[:, 512:], tn)
    return lo, gt, grad_gate, grad_up, gd.reshape(2048, 256).astype(F32)


def solution(mesh):
    ins = (P("gy", ("gz", "gx")), P("gy", ("gz", "gx")), P("gz", ("gx", "gy")),
           P("gz", ("gx", "gy")), P("gx", ("gz", "gy")))
    outs = (P("gy", ("gz", "gx")), P("gy", ("gz", "gx")), P("gz", ("gx", "gy")),
            P("gz", ("gx", "gy")), P("gx", ("gz", "gy")))
    return jax.shard_map(local, mesh=mesh, in_specs=ins, out_specs=outs, check_vma=False)
```

```python
import jax
import jax.numpy as jnp
from jax import lax
from jax.experimental import pallas as pl
from jax.experimental.pallas import tpu as pltpu
from jax.sharding import PartitionSpec as P

MESH = pl.DeviceIdType.MESH
BF, F32 = jnp.bfloat16, jnp.float32
XT = jnp.bfloat16
YT = jnp.float32
NSEM = 256
PARTS = (2, 1, 1, 2)
TPARTS = 2


def dot(a, b, dims):
    return lax.dot_general(a, b, (dims, ((), ())), preferred_element_type=F32)


class Net:
    def __init__(self, send, recv):
        self.send, self.recv, self.used, self.out = send, recv, 0, []

    def slot(self):
        self.used += 1
        return self.used - 1

    def push(self, src, dst, device, k=None):
        k = self.slot() if k is None else k
        copy = pltpu.make_async_remote_copy(
            src_ref=src, dst_ref=dst, send_sem=self.send.at[k], recv_sem=self.recv.at[k],
            device_id=device, device_id_type=MESH)
        copy.start()
        self.out.append(copy)
        return k

    def local(self, src, dst):
        k = self.slot()
        copy = pltpu.make_async_copy(src, dst, self.recv.at[k])
        copy.start()
        return copy

    def arrived(self, k, landing):
        pltpu.make_async_copy(landing, landing, self.recv.at[k]).wait()

    def drain(self):
        for copy in self.out:
            copy.wait_send()
        self.out = []


class ReduceScatter:
    def __init__(self, net, part, sent, half, full, rows, pos, plus, minus):
        self.net, self.part, self.sent, self.half, self.full = net, part, sent, half, full
        self.rows, self.pos, self.plus, self.minus = rows, pos, plus, minus

    def start(self):
        m = self.rows // 2
        far = self.sent(0, 0, self.rows)
        far[...] = self.part((self.pos + 2) % 4, 0, self.rows)[...].astype(far.dtype)
        self.ka = self.net.push(self.sent(0, 0, m), self.half(0), self.plus)
        self.kb = self.net.push(self.sent(0, m, m), self.half(1), self.minus)

    def middle(self):
        m = self.rows // 2
        right, left = (self.pos + 1) % 4, (self.pos + 3) % 4
        net, part, sent, half = self.net, self.part, self.sent, self.half
        kind = half(0).dtype
        sent(1, m, m)[...] = part(right, m, m)[...].astype(kind)
        sent(2, 0, m)[...] = part(left, 0, m)[...].astype(kind)
        net.arrived(self.ka, half(0))
        sent(1, 0, m)[...] = (part(right, 0, m)[...] + half(0)[...].astype(F32)).astype(kind)
        self.kp = net.push(sent(1, 0, self.rows), self.full(0), self.plus)
        net.arrived(self.kb, half(1))
        sent(2, m, m)[...] = (part(left, m, m)[...] + half(1)[...].astype(F32)).astype(kind)
        self.km = net.push(sent(2, 0, self.rows), self.full(1), self.minus)

    def finish(self):
        self.net.arrived(self.kp, self.full(0))
        self.net.arrived(self.km, self.full(1))
        return (self.part(self.pos, 0, self.rows)[...] + self.full(0)[...].astype(F32)
                + self.full(1)[...].astype(F32))


class AllGather:
    def __init__(self, net, slot, rows, pos, plus, minus):
        self.net, self.slot, self.rows = net, slot, rows
        self.pos, self.plus, self.minus = pos, plus, minus

    def start(self):
        own = self.slot(self.pos, 0, self.rows)
        self.kp = self.net.push(own, own, self.plus)
        self.km = self.net.push(own, own, self.minus)

    def forward(self):
        m = self.rows // 2
        right, left = (self.pos + 1) % 4, (self.pos + 3) % 4
        self.net.arrived(self.kp, self.slot(left, 0, self.rows))
        first = self.slot(left, 0, m)
        self.ka = self.net.push(first, first, self.plus)
        self.net.arrived(self.km, self.slot(right, 0, self.rows))
        second = self.slot(right, m, m)
        self.kb = self.net.push(second, second, self.minus)

    def finish(self):
        m = self.rows // 2
        far = (self.pos + 2) % 4
        self.net.arrived(self.ka, self.slot(far, 0, m))
        self.net.arrived(self.kb, self.slot(far, m, m))


def kernel(tok, cot, wg, wu, wd, lo, gt, t_out, g_out, gd_out,
           T, C, W, V, H, G, PG, PH, GU, sg, hg, fg, sh, hh, fh,
           own, give, take, sx, hx, fx, sy, ry, gs, gr, send, recv):
    gx, gy, gz = lax.axis_index("gx"), lax.axis_index("gy"), lax.axis_index("gz")
    x, z, c = gx // 2, gz, gy % 2
    yh, yl = gy // 2, gx % 2
    y = yh * 2 + yl

    def at(x, y, z, c):
        return (x * 2 + y % 2, (y // 2) * 2 + c, z)

    def span(start, size):
        return pl.ds(pl.multiple_of(start, size), size)

    ys = [at(x, (y + d) % 4, z, c) for d in (1, 2, 3)]
    xs = [at((x + d) % 4, y, z, c) for d in (1, 2, 3)]
    zp, zm = at(x, y, (z + 1) % 4, c), at(x, y, (z + 3) % 4, c)
    mate = at(x, y, z, 1 - c)
    cross = at(x, (y + 2) % 4, z, 1 - c)
    net = Net(send, recv)

    loads = [net.local(tok, T.at[gy, :, span(gx * 128, 128)]),
             net.local(cot, C.at[gy, :, span(gx * 128, 128)])]
    w_loads = [net.local(wg, W.at[:, pl.ds(0, 512)]), net.local(wu, W.at[:, pl.ds(512, 512)])]
    v_load = net.local(wd.at[span(gy * 512, 512)], V.at[:, span(gy * 256, 256)])

    barrier = pltpu.get_barrier_semaphore()
    peers = ys + xs + [zp, zm, mate, cross]
    for peer in peers:
        pl.semaphore_signal(barrier, inc=1, device_id=peer, device_id_type=MESH)
    pl.semaphore_wait(barrier, len(peers))

    waits = {}

    def need(*keys):
        for key in keys:
            if key in waits:
                waits.pop(key)()

    def gather_y(src, buf, r, n):
        rows = pl.ds(r * n, n)
        mine = buf.at[gy, rows, span(gx * 128, 128)]
        ks = [net.push(src.at[rows], mine, d) for d in ys]

        def done():
            for d, k in zip((3, 2, 1), ks):
                yy = (y + d) % 4
                net.arrived(k, buf.at[(yy // 2) * 2 + c, rows, span((x * 2 + yy % 2) * 128, 128)])
        return done

    def gather_x(buf, h, r, n):
        rows = pl.ds(r * n, n)
        mine = buf.at[h * 2 + c, rows, span(x * 256, 256)]
        ks = [net.push(mine, mine, d) for d in xs]

        def done():
            for d, k in zip((3, 2, 1), ks):
                net.arrived(k, buf.at[h * 2 + c, rows, span(((x + d) % 4) * 256, 256)])
        return done

    def share(buf, h):
        mine = buf.at[h * 2 + c]
        k = net.push(mine, mine, mate)
        return lambda: net.arrived(k, buf.at[h * 2 + 1 - c])

    chunk = [c, 1 - c, 2 + 1 - c, 2 + c]
    parts = [(i, r) for i in range(4) for r in range(PARTS[i])]
    rs_g, rs_h, ag_h, ag_g, rs_x = {}, {}, {}, {}, {}

    def ring_z(i, r, P, s, h, f):
        n = 256 // PARTS[i]
        q = n // 4
        return ReduceScatter(
            net, lambda k, a, m: P.at[i, span(r * n + k * q + a, m)],
            lambda k, a, m: s.at[i, k, pl.ds(r * q + a, m)],
            lambda k: h.at[i, k, pl.ds(r * q // 2, q // 2)],
            lambda k: f.at[i, k, pl.ds(r * q, q)], q, z, zp, zm)

    def gather_z(i, r, B):
        n = 256 // PARTS[i]
        q = n // 4
        return AllGather(net, lambda k, a, m: B.at[chunk[i], span(r * n + k * q + a, m)], q, z, zp, zm)

    def ring_x(m, o, r, n):
        return ReduceScatter(
            net, lambda k, a, l: own.at[m, o, k, pl.ds(r * n + a, l)],
            lambda k, a, l: sx.at[m, o, k, pl.ds(r * n + a, l)],
            lambda k: hx.at[m, o, k, pl.ds(r * n // 2, n // 2)],
            lambda k: fx.at[m, o, k, pl.ds(r * n, n)], n, x, xs[0], xs[2])

    for i, r in parts:
        rs_g[i, r] = ring_z(i, r, PG, sg, hg, fg)
        rs_h[i, r] = ring_z(i, r, PH, sh, hh, fh)
        ag_h[i, r] = gather_z(i, r, H)
        ag_g[i, r] = gather_z(i, r, G)
        if i in (0, 3):
            for m in range(2):
                rs_x[m, i // 3, r] = ring_x(m, i // 3, r, 256 // PARTS[i])

    def rows_of(i, r):
        n = 256 // PARTS[i]
        return pl.ds(r * n, n)

    def quarter(i, r):
        q = 64 // PARTS[i]
        return pl.ds(r * q, q)

    def all_of(copies):
        return lambda: [copy.wait() for copy in copies]

    waits["own"], waits["weights"] = all_of(loads), all_of(w_loads)

    def ty(r):
        waits["ty", r] = gather_y(tok, T, r, 256 // TPARTS)

    def tx(h, r):
        need("own", ("ty", r))
        waits["tx", h, r] = gather_x(T, h, r, 256 // TPARTS)

    def tm(h):
        need(*[("tx", h, r) for r in range(TPARTS)])
        waits["tm", h] = share(T, h)

    def cy():
        waits["cy"] = gather_y(cot, C, 0, 256)

    def cx(h):
        need("own", "cy")
        waits["cx", h] = gather_x(C, h, 0, 256)

    def cm(h):
        need(("cx", h))
        waits["cm", h] = share(C, h)

    def v():
        waits["v"] = down_share()

    def save(src, dst):
        keep.append(net.local(src, dst))

    def g1(i, r):
        need("weights")
        if i in (0, 3):
            need(*[("tx", i // 3, q) for q in ([r] if TPARTS == PARTS[i] else range(TPARTS))])
        else:
            need(("tm", i - 1))
        PG[i, rows_of(i, r)] = dot(T[chunk[i], rows_of(i, r)], W[...], ((1,), (0,)))
        rs_g[i, r].start()

    def g2(i, r):
        rs_g[i, r].middle()

    def g3(i, r):
        s = rs_g[i, r].finish()
        GU[i, quarter(i, r)] = s
        gate, up = s[:, :512], s[:, 512:]
        gather = ag_h[i, r]
        gather.slot(z, 0, gather.rows)[...] = (gate * jax.nn.sigmoid(gate) * up).astype(BF)
        gather.start()

    def g4(i, r):
        ag_h[i, r].forward()

    def h1(i, r):
        need("v", ("cx", i // 3) if i in (0, 3) else ("cm", i - 1))
        PH[i, rows_of(i, r)] = dot(C[chunk[i], rows_of(i, r)], V[...], ((1,), (1,)))
        rs_h[i, r].start()

    def h2(i, r):
        rs_h[i, r].middle()

    def h3(i, r):
        grad = rs_h[i, r].finish()
        gate, up = GU[i, quarter(i, r), :512], GU[i, quarter(i, r), 512:]
        s = jax.nn.sigmoid(gate)
        gather = ag_g[i, r]
        slot = gather.slot(z, 0, gather.rows)
        slot[:, :512] = (grad * up * s * (1.0 + gate * (1.0 - s))).astype(BF)
        slot[:, 512:] = (grad * (gate * s)).astype(BF)
        gather.start()

    def h4(i, r):
        ag_g[i, r].forward()

    took = {}

    def place(m, i, r, part):
        dst = (own.at[m, 0], give.at[m, 0], give.at[m, 1], own.at[m, 1])[i]
        rows = rows_of(i, r)
        for n in range(4):
            dst[n, rows] = part[:, n * 256:n * 256 + 256]
        if i in (1, 2):
            there = take.at[m, i - 1, :, rows]
            took[m, i - 1, r] = net.push(dst.at[:, rows], there, mate), there

    def g5(i, r):
        need("v")
        ag_h[i, r].finish()
        place(0, i, r, dot(H[chunk[i], rows_of(i, r)], V[...], ((1,), (0,))))

    def h5(i, r):
        ag_g[i, r].finish()
        place(1, i, r, dot(G[chunk[i], rows_of(i, r)], W[...], ((1,), (1,))))
        if all((h5, i, q) in ran or q == r for q in range(PARTS[i])):
            save(G.at[chunk[i]], g_out.at[chunk[i]])

    def x1(m, i, r):
        o = i // 3
        if PARTS[1 + o] == PARTS[i]:
            keys = [r]
        else:
            keys = range(PARTS[1 + o])
        for q in keys:
            if (m, o, q) in took:
                net.arrived(*took.pop((m, o, q)))
        rows = rows_of(i, r)
        for n in range(4):
            own[m, o, n, rows] += take[m, o, n, rows]
        rs_x[m, o, r].start()

    def x2(m, i, r):
        rs_x[m, i // 3, r].middle()

    ky = {(m, i // 3, r): [net.slot() for _ in range(3)] for m in range(2) for i, r in parts if i in (0, 3)}

    def y_copy(m, i, r, t, d):
        o, rows = i // 3, rows_of(i, r)
        k = ky[m, o, r][d - 1]
        return pltpu.make_async_remote_copy(
            src_ref=sy.at[m, o, t, rows], dst_ref=ry.at[m, d - 1, rows],
            send_sem=send.at[k], recv_sem=recv.at[k],
            device_id=at(x, 2 * o + t, z, c), device_id_type=MESH)

    def x3(m, i, r):
        o, rows = i // 3, rows_of(i, r)
        total = rs_x[m, o, r].finish()
        sy[m, o, 0, rows] = total[:, :128].astype(YT)
        sy[m, o, 1, rows] = total[:, 128:].astype(YT)
        for t in range(2):
            for d in (1, 2, 3):
                @pl.when((y + d) % 4 == 2 * o + t)
                def _():
                    y_copy(m, i, r, t, d).start()

    def y_sent(m, i, r):
        for t in range(2):
            for d in (1, 2, 3):
                @pl.when((y + d) % 4 == 2 * (i // 3) + t)
                def _():
                    y_copy(m, i, r, t, d).wait_send()

    def y_all(m):
        for i, r in parts:
            if i in (0, 3):
                @pl.when(yh == i // 3)
                def _():
                    rows = rows_of(i, r)
                    total = sy[m, i // 3, yl, rows].astype(F32)
                    for d in (1, 2, 3):
                        net.arrived(ky[m, i // 3, r][d - 1], ry.at[m, d - 1, rows])
                        total += ry[m, d - 1, rows].astype(F32)
                    (lo, gt)[m][rows] = total.astype(BF)

    others = [((1 - yh) * 2 + c, ys[1]), ((1 - yh) * 2 + 1 - c, cross), (yh * 2 + 1 - c, mate)]
    gk = []

    def down_grad():
        need(("cx", 0), ("cx", 1), ("cm", 0), ("cm", 1))
        part = dot(H[...].reshape(1024, 512), C[...].reshape(1024, 1024), ((0,), (0,))).astype(BF)
        for g in range(4):
            gs[g] = part[:, g * 256:g * 256 + 256]
        gk.extend((net.push(gs.at[g], gr.at[gy], device), g) for g, device in others)
        gr[gy] = gs[gy]

    def down_done():
        for k, g in gk:
            net.arrived(k, gr.at[g])
        save(gr, gd_out)

    def down_share():
        dst = V.at[:, span(gy * 256, 256)]
        ks = [(net.push(wd.at[span(g * 512, 512)], dst, device), g) for g, device in others]

        def done():
            for k, g in ks:
                net.arrived(k, V.at[:, span(g * 256, 256)])
            v_load.wait()
        return done

    keep, ran = [], set()

    steps = [
        (ty, 0), (ty, 1), (cy,), (tx, 1, 0), (tx, 0, 0), (tx, 0, 1), (tx, 1, 1), (g1, 3, 0),
        (g1, 0, 0), (g2, 3, 0), (g1, 0, 1), (g2, 0, 0), (g3, 3, 0), (v,), (tm, 1), (g2, 0, 1),
        (tm, 0), (g1, 3, 1), (cx, 1), (g3, 0, 0), (g1, 2, 0), (g1, 1, 0), (g4, 0, 0), (cx, 0),
        (g2, 3, 1), (g2, 2, 0), (g3, 3, 1), (g2, 1, 0), (cm, 1), (g3, 2, 0), (g3, 0, 1), (g4, 3, 1),
        (cm, 0), (h1, 2, 0), (g4, 3, 0), (g3, 1, 0), (g4, 2, 0), (h1, 3, 0), (h2, 2, 0), (h1, 0, 1),
        (h1, 1, 0), (g4, 1, 0), (h1, 0, 0), (g5, 3, 0), (g5, 2, 0), (g4, 0, 1), (h2, 3, 0),
        (h3, 2, 0), (h2, 1, 0), (g5, 1, 0), (g5, 0, 0), (h1, 3, 1), (x1, 0, 3, 0), (h2, 0, 1),
        (g5, 0, 1), (h4, 2, 0), (x1, 0, 0, 0), (h3, 3, 0), (g5, 3, 1), (x1, 0, 3, 1), (x1, 0, 0, 1),
        (h3, 1, 0), (down_grad,), (h5, 2, 0), (h4, 3, 0), (h2, 3, 1), (x2, 0, 0, 1), (x2, 0, 0, 0),
        (h3, 0, 1), (x2, 0, 3, 1), (h2, 0, 0), (h4, 1, 0), (h5, 3, 0), (h3, 3, 1), (x1, 1, 3, 0),
        (h3, 0, 0), (h4, 0, 1), (x3, 0, 0, 0), (h5, 1, 0), (x2, 0, 3, 0), (x3, 0, 0, 1), (h4, 3, 1),
        (x3, 0, 3, 1), (x2, 1, 3, 0), (h4, 0, 0), (h5, 0, 1), (x1, 1, 0, 1), (h5, 3, 1),
        (x1, 1, 3, 1), (h5, 0, 0), (x1, 1, 0, 0), (x3, 0, 3, 0), (x2, 1, 0, 1), (x2, 1, 3, 1),
        (x3, 1, 3, 0), (down_done,), (x2, 1, 0, 0), (x3, 1, 0, 1), (y_all, 0), (x3, 1, 3, 1),
        (x3, 1, 0, 0), (y_all, 1),
    ]
    for f, *args in steps:
        f(*args)
        ran.add((f, *args))
        if f is tm and len([s for s in ran if s[0] is tm]) == 2:
            need(("tm", 0), ("tm", 1))
            save(T, t_out)
    for copy in keep:
        copy.wait()
    for m in range(2):
        for i, r in parts:
            if i in (0, 3):
                y_sent(m, i, r)
    net.drain()


def local(tok, cot, wg, wu, wd):
    any_, vmem = pl.BlockSpec(memory_space=pl.ANY), pl.BlockSpec(memory_space=pltpu.VMEM)
    S = jax.ShapeDtypeStruct
    scratch = [
        pltpu.VMEM((4, 256, 1024), BF),
        pltpu.VMEM((4, 256, 1024), BF),
        pltpu.VMEM((1024, 1024), BF),
        pltpu.VMEM((512, 1024), BF),
        pltpu.VMEM((4, 256, 512), BF),
        pltpu.VMEM((4, 256, 1024), BF),
        pltpu.VMEM((4, 256, 1024), F32),
        pltpu.VMEM((4, 256, 512), F32),
        pltpu.VMEM((4, 64, 1024), F32),
        pltpu.VMEM((4, 3, 64, 1024), BF),
        pltpu.VMEM((4, 2, 32, 1024), BF),
        pltpu.VMEM((4, 2, 64, 1024), BF),
        pltpu.VMEM((4, 3, 64, 512), BF),
        pltpu.VMEM((4, 2, 32, 512), BF),
        pltpu.VMEM((4, 2, 64, 512), BF),
        pltpu.VMEM((2, 2, 4, 256, 256), F32),
        pltpu.VMEM((2, 2, 4, 256, 256), F32),
        pltpu.VMEM((2, 2, 4, 256, 256), F32),
        pltpu.VMEM((2, 2, 3, 256, 256), XT),
        pltpu.VMEM((2, 2, 2, 128, 256), XT),
        pltpu.VMEM((2, 2, 2, 256, 256), XT),
        pltpu.VMEM((2, 2, 2, 256, 128), YT),
        pltpu.VMEM((2, 3, 256, 128), YT),
        pltpu.VMEM((4, 512, 256), BF),
        pltpu.VMEM((4, 512, 256), BF),
        pltpu.SemaphoreType.DMA((NSEM,)),
        pltpu.SemaphoreType.DMA((NSEM,)),
    ]
    lo, gt, t_all, g_all, gd = pl.pallas_call(
        kernel,
        out_shape=[S((256, 128), BF), S((256, 128), BF), S((4, 256, 1024), BF),
                   S((4, 256, 1024), BF), S((4, 512, 256), BF)],
        in_specs=[any_] * 5,
        out_specs=[vmem, vmem, any_, any_, any_],
        scratch_shapes=scratch,
        compiler_params=pltpu.CompilerParams(
            collective_id=0, has_side_effects=True, vmem_limit_bytes=56 << 20),
        cost_estimate=pl.CostEstimate(flops=8_000_000_000, bytes_accessed=10_000_000, transcendentals=600_000),
        name="layer",
    )(tok, cot, wg, wu, wd)
    return weight_grads(lo, gt, t_all.reshape(1024, 1024), g_all.reshape(1024, 1024), gd.reshape(2048, 256))


def weight_grads_kernel(lo, gt, t_in, g_in, gd_in, lo_out, gt_out, gg_out, gu_out, gd_out, T, G, D, gg, gu, gd, sems):
    count = [0]

    def copy(src, dst):
        made = pltpu.make_async_copy(src, dst, sems.at[count[0]])
        count[0] += 1
        made.start()
        return made

    blocks = [pl.ds(n * 256, 256) for n in range(4)]
    first = [copy(g_in.at[rows], G.at[rows]) for rows in blocks]
    t_loads = [copy(t_in.at[:, cols], T.at[:, cols]) for cols in blocks]
    d_loads = [copy(gd_in.at[pl.ds(n * 1024, 1024)], D.at[pl.ds(n * 1024, 1024)]) for n in range(2)]
    small = [copy(lo, lo_out), copy(gt, gt_out)]
    for load in first:
        load.wait()
    stores = []
    for n in range(4):
        rows = blocks[n]
        t_loads[n].wait()
        part = dot(T[:, rows], G[...], ((0,), (0,)))
        gg[rows] = part[:, :512]
        stores.append(copy(gg.at[rows], gg_out.at[rows]))
        gu[rows] = part[:, 512:]
        stores.append(copy(gu.at[rows], gu_out.at[rows]))
        if n < 2:
            rows = pl.ds(n * 1024, 1024)
            d_loads[n].wait()
            gd[rows] = D[rows].astype(F32)
            stores.append(copy(gd.at[rows], gd_out.at[rows]))
    for made in stores + small:
        made.wait()


def weight_grads(lo, gt, t_all, g_all, gd):
    any_ = pl.BlockSpec(memory_space=pl.ANY)
    S = jax.ShapeDtypeStruct
    return pl.pallas_call(
        weight_grads_kernel,
        out_shape=[S((256, 128), BF), S((256, 128), BF), S((1024, 512), F32), S((1024, 512), F32),
                   S((2048, 256), F32)],
        in_specs=[any_] * 5,
        out_specs=[any_] * 5,
        scratch_shapes=[
            pltpu.VMEM((1024, 1024), BF), pltpu.VMEM((1024, 1024), BF), pltpu.VMEM((2048, 256), BF),
            pltpu.VMEM((1024, 512), F32), pltpu.VMEM((1024, 512), F32), pltpu.VMEM((2048, 256), F32),
            pltpu.SemaphoreType.DMA((24,))],
        compiler_params=pltpu.CompilerParams(vmem_limit_bytes=60 << 20),
        cost_estimate=pl.CostEstimate(flops=2_200_000_000, bytes_accessed=12_000_000, transcendentals=0),
        name="weight_grads",
    )(lo, gt, t_all, g_all, gd)


def solution(mesh):
    ins = (P("gy", ("gz", "gx")), P("gy", ("gz", "gx")), P("gz", ("gx", "gy")),
           P("gz", ("gx", "gy")), P("gx", ("gz", "gy")))
    outs = (P("gy", ("gz", "gx")), P("gy", ("gz", "gx")), P("gz", ("gx", "gy")),
            P("gz", ("gx", "gy")), P("gx", ("gz", "gy")))
    return jax.shard_map(local, mesh=mesh, in_specs=ins, out_specs=outs, check_vma=False)
```

```python
import jax
import jax.numpy as jnp
from jax import lax
from jax.experimental import pallas as pl
from jax.experimental.pallas import tpu as pltpu
from jax.sharding import PartitionSpec as P

MESH = pl.DeviceIdType.MESH
BF, F32 = jnp.bfloat16, jnp.float32
XT = jnp.bfloat16
YT = jnp.bfloat16
NSEM = 256
PARTS = (2, 1, 1, 2)
TPARTS = 2


def dot(a, b, dims):
    return lax.dot_general(a, b, (dims, ((), ())), preferred_element_type=F32)


class Net:
    def __init__(self, send, recv):
        self.send, self.recv, self.used, self.out = send, recv, 0, []

    def slot(self):
        self.used += 1
        return self.used - 1

    def push(self, src, dst, device, k=None):
        k = self.slot() if k is None else k
        copy = pltpu.make_async_remote_copy(
            src_ref=src, dst_ref=dst, send_sem=self.send.at[k], recv_sem=self.recv.at[k],
            device_id=device, device_id_type=MESH)
        copy.start()
        self.out.append(copy)
        return k

    def local(self, src, dst):
        k = self.slot()
        copy = pltpu.make_async_copy(src, dst, self.recv.at[k])
        copy.start()
        return copy

    def arrived(self, k, landing):
        pltpu.make_async_copy(landing, landing, self.recv.at[k]).wait()

    def drain(self):
        for copy in self.out:
            copy.wait_send()
        self.out = []


class ReduceScatter:
    def __init__(self, net, part, sent, half, full, rows, pos, plus, minus):
        self.net, self.part, self.sent, self.half, self.full = net, part, sent, half, full
        self.rows, self.pos, self.plus, self.minus = rows, pos, plus, minus

    def start(self):
        m = self.rows // 2
        far = self.sent(0, 0, self.rows)
        far[...] = self.part((self.pos + 2) % 4, 0, self.rows)[...].astype(far.dtype)
        self.ka = self.net.push(self.sent(0, 0, m), self.half(0), self.plus)
        self.kb = self.net.push(self.sent(0, m, m), self.half(1), self.minus)

    def middle(self):
        m = self.rows // 2
        right, left = (self.pos + 1) % 4, (self.pos + 3) % 4
        net, part, sent, half = self.net, self.part, self.sent, self.half
        kind = half(0).dtype
        sent(1, m, m)[...] = part(right, m, m)[...].astype(kind)
        sent(2, 0, m)[...] = part(left, 0, m)[...].astype(kind)
        net.arrived(self.ka, half(0))
        sent(1, 0, m)[...] = (part(right, 0, m)[...] + half(0)[...].astype(F32)).astype(kind)
        self.kp = net.push(sent(1, 0, self.rows), self.full(0), self.plus)
        net.arrived(self.kb, half(1))
        sent(2, m, m)[...] = (part(left, m, m)[...] + half(1)[...].astype(F32)).astype(kind)
        self.km = net.push(sent(2, 0, self.rows), self.full(1), self.minus)

    def finish(self):
        self.net.arrived(self.kp, self.full(0))
        self.net.arrived(self.km, self.full(1))
        return (self.part(self.pos, 0, self.rows)[...] + self.full(0)[...].astype(F32)
                + self.full(1)[...].astype(F32))


class AllGather:
    def __init__(self, net, slot, rows, pos, plus, minus):
        self.net, self.slot, self.rows = net, slot, rows
        self.pos, self.plus, self.minus = pos, plus, minus

    def start(self):
        own = self.slot(self.pos, 0, self.rows)
        self.kp = self.net.push(own, own, self.plus)
        self.km = self.net.push(own, own, self.minus)

    def forward(self):
        m = self.rows // 2
        right, left = (self.pos + 1) % 4, (self.pos + 3) % 4
        self.net.arrived(self.kp, self.slot(left, 0, self.rows))
        first = self.slot(left, 0, m)
        self.ka = self.net.push(first, first, self.plus)
        self.net.arrived(self.km, self.slot(right, 0, self.rows))
        second = self.slot(right, m, m)
        self.kb = self.net.push(second, second, self.minus)

    def finish(self):
        m = self.rows // 2
        far = (self.pos + 2) % 4
        self.net.arrived(self.ka, self.slot(far, 0, m))
        self.net.arrived(self.kb, self.slot(far, m, m))


def kernel(tok, cot, wg, wu, wd, lo, gt, t_out, g_out, gd_out,
           T, C, W, V, H, G, PG, PH, GU, sg, hg, fg, sh, hh, fh,
           own, give, take, sx, hx, fx, sy, ry, mine, gs, gr, send, recv):
    gx, gy, gz = lax.axis_index("gx"), lax.axis_index("gy"), lax.axis_index("gz")
    x, z, c = gx // 2, gz, gy % 2
    yh, yl = gy // 2, gx % 2
    y = yh * 2 + yl

    def at(x, y, z, c):
        return (x * 2 + y % 2, (y // 2) * 2 + c, z)

    def span(start, size):
        return pl.ds(pl.multiple_of(start, size), size)

    ys = [at(x, (y + d) % 4, z, c) for d in (1, 2, 3)]
    xs = [at((x + d) % 4, y, z, c) for d in (1, 2, 3)]
    zp, zm = at(x, y, (z + 1) % 4, c), at(x, y, (z + 3) % 4, c)
    mate = at(x, y, z, 1 - c)
    cross = at(x, (y + 2) % 4, z, 1 - c)
    net = Net(send, recv)

    loads = [net.local(tok, T.at[gy, :, span(gx * 128, 128)]),
             net.local(cot, C.at[gy, :, span(gx * 128, 128)])]
    w_loads = [net.local(wg, W.at[:, pl.ds(0, 512)]), net.local(wu, W.at[:, pl.ds(512, 512)])]
    v_load = net.local(wd.at[span(gy * 512, 512)], V.at[:, span(gy * 256, 256)])

    barrier = pltpu.get_barrier_semaphore()
    peers = ys + xs + [zp, zm, mate, cross]
    for peer in peers:
        pl.semaphore_signal(barrier, inc=1, device_id=peer, device_id_type=MESH)
    pl.semaphore_wait(barrier, len(peers))

    waits = {}

    def need(*keys):
        for key in keys:
            if key in waits:
                waits.pop(key)()

    def gather_y(src, buf, r, n):
        rows = pl.ds(r * n, n)
        mine = buf.at[gy, rows, span(gx * 128, 128)]
        ks = [net.push(src.at[rows], mine, d) for d in ys]

        def done():
            for d, k in zip((3, 2, 1), ks):
                yy = (y + d) % 4
                net.arrived(k, buf.at[(yy // 2) * 2 + c, rows, span((x * 2 + yy % 2) * 128, 128)])
        return done

    def gather_x(buf, h, r, n):
        rows = pl.ds(r * n, n)
        mine = buf.at[h * 2 + c, rows, span(x * 256, 256)]
        ks = [net.push(mine, mine, d) for d in xs]

        def done():
            for d, k in zip((3, 2, 1), ks):
                net.arrived(k, buf.at[h * 2 + c, rows, span(((x + d) % 4) * 256, 256)])
        return done

    def share(buf, h):
        mine = buf.at[h * 2 + c]
        k = net.push(mine, mine, mate)
        return lambda: net.arrived(k, buf.at[h * 2 + 1 - c])

    chunk = [c, 1 - c, 2 + 1 - c, 2 + c]
    parts = [(i, r) for i in range(4) for r in range(PARTS[i])]
    rs_g, rs_h, ag_h, ag_g, rs_x = {}, {}, {}, {}, {}

    def ring_z(i, r, P, s, h, f):
        n = 256 // PARTS[i]
        q = n // 4
        return ReduceScatter(
            net, lambda k, a, m: P.at[i, span(r * n + k * q + a, m)],
            lambda k, a, m: s.at[i, k, pl.ds(r * q + a, m)],
            lambda k: h.at[i, k, pl.ds(r * q // 2, q // 2)],
            lambda k: f.at[i, k, pl.ds(r * q, q)], q, z, zp, zm)

    def gather_z(i, r, B):
        n = 256 // PARTS[i]
        q = n // 4
        return AllGather(net, lambda k, a, m: B.at[chunk[i], span(r * n + k * q + a, m)], q, z, zp, zm)

    def ring_x(m, o, r, n):
        return ReduceScatter(
            net, lambda k, a, l: own.at[m, o, k, pl.ds(r * n + a, l)],
            lambda k, a, l: sx.at[m, o, k, pl.ds(r * n + a, l)],
            lambda k: hx.at[m, o, k, pl.ds(r * n // 2, n // 2)],
            lambda k: fx.at[m, o, k, pl.ds(r * n, n)], n, x, xs[0], xs[2])

    for i, r in parts:
        rs_g[i, r] = ring_z(i, r, PG, sg, hg, fg)
        rs_h[i, r] = ring_z(i, r, PH, sh, hh, fh)
        ag_h[i, r] = gather_z(i, r, H)
        ag_g[i, r] = gather_z(i, r, G)
        if i in (0, 3):
            for m in range(2):
                rs_x[m, i // 3, r] = ring_x(m, i // 3, r, 256 // PARTS[i])

    def rows_of(i, r):
        n = 256 // PARTS[i]
        return pl.ds(r * n, n)

    def quarter(i, r):
        q = 64 // PARTS[i]
        return pl.ds(r * q, q)

    def all_of(copies):
        return lambda: [copy.wait() for copy in copies]

    waits["own"], waits["weights"] = all_of(loads), all_of(w_loads)

    def ty(r):
        waits["ty", r] = gather_y(tok, T, r, 256 // TPARTS)

    def tx(h, r):
        need("own", ("ty", r))
        waits["tx", h, r] = gather_x(T, h, r, 256 // TPARTS)

    def tm(h):
        need(*[("tx", h, r) for r in range(TPARTS)])
        waits["tm", h] = share(T, h)

    def cy():
        waits["cy"] = gather_y(cot, C, 0, 256)

    def cx(h):
        need("own", "cy")
        waits["cx", h] = gather_x(C, h, 0, 256)

    def cm(h):
        need(("cx", h))
        waits["cm", h] = share(C, h)

    def v():
        waits["v"] = down_share()

    def save(src, dst):
        keep.append(net.local(src, dst))

    def g1(i, r):
        need("weights")
        if i in (0, 3):
            need(*[("tx", i // 3, q) for q in ([r] if TPARTS == PARTS[i] else range(TPARTS))])
        else:
            need(("tm", i - 1))
        PG[i, rows_of(i, r)] = dot(T[chunk[i], rows_of(i, r)], W[...], ((1,), (0,)))
        rs_g[i, r].start()

    def g2(i, r):
        rs_g[i, r].middle()

    def g3(i, r):
        s = rs_g[i, r].finish()
        GU[i, quarter(i, r)] = s
        gate, up = s[:, :512], s[:, 512:]
        gather = ag_h[i, r]
        gather.slot(z, 0, gather.rows)[...] = (gate * jax.nn.sigmoid(gate) * up).astype(BF)
        gather.start()

    def g4(i, r):
        ag_h[i, r].forward()

    def h1(i, r):
        need("v", ("cx", i // 3) if i in (0, 3) else ("cm", i - 1))
        PH[i, rows_of(i, r)] = dot(C[chunk[i], rows_of(i, r)], V[...], ((1,), (1,)))
        rs_h[i, r].start()

    def h2(i, r):
        rs_h[i, r].middle()

    def h3(i, r):
        grad = rs_h[i, r].finish()
        gate, up = GU[i, quarter(i, r), :512], GU[i, quarter(i, r), 512:]
        s = jax.nn.sigmoid(gate)
        gather = ag_g[i, r]
        slot = gather.slot(z, 0, gather.rows)
        slot[:, :512] = (grad * up * s * (1.0 + gate * (1.0 - s))).astype(BF)
        slot[:, 512:] = (grad * (gate * s)).astype(BF)
        gather.start()

    def h4(i, r):
        ag_g[i, r].forward()

    took = {}

    def place(m, i, r, part):
        dst = (own.at[m, 0], give.at[m, 0], give.at[m, 1], own.at[m, 1])[i]
        rows = rows_of(i, r)
        for n in range(4):
            dst[n, rows] = part[:, n * 256:n * 256 + 256]
        if i in (1, 2):
            there = take.at[m, i - 1, :, rows]
            took[m, i - 1, r] = net.push(dst.at[:, rows], there, mate), there

    def g5(i, r):
        need("v")
        ag_h[i, r].finish()
        place(0, i, r, dot(H[chunk[i], rows_of(i, r)], V[...], ((1,), (0,))))

    def h5(i, r):
        ag_g[i, r].finish()
        place(1, i, r, dot(G[chunk[i], rows_of(i, r)], W[...], ((1,), (1,))))
        if all((h5, i, q) in ran or q == r for q in range(PARTS[i])):
            save(G.at[chunk[i]], g_out.at[chunk[i]])

    def x1(m, i, r):
        o = i // 3
        if PARTS[1 + o] == PARTS[i]:
            keys = [r]
        else:
            keys = range(PARTS[1 + o])
        for q in keys:
            if (m, o, q) in took:
                net.arrived(*took.pop((m, o, q)))
        rows = rows_of(i, r)
        for n in range(4):
            own[m, o, n, rows] += take[m, o, n, rows]
        rs_x[m, o, r].start()

    def x2(m, i, r):
        rs_x[m, i // 3, r].middle()

    ky = {(m, i // 3, r): [net.slot() for _ in range(3)] for m in range(2) for i, r in parts if i in (0, 3)}

    def y_copy(m, i, r, t, d):
        o, rows = i // 3, rows_of(i, r)
        k = ky[m, o, r][d - 1]
        return pltpu.make_async_remote_copy(
            src_ref=sy.at[m, o, t, rows], dst_ref=ry.at[m, d - 1, rows],
            send_sem=send.at[k], recv_sem=recv.at[k],
            device_id=at(x, 2 * o + t, z, c), device_id_type=MESH)

    def x3(m, i, r):
        o, rows = i // 3, rows_of(i, r)
        total = rs_x[m, o, r].finish()
        sy[m, o, 0, rows] = total[:, :128].astype(YT)
        sy[m, o, 1, rows] = total[:, 128:].astype(YT)

        @pl.when(y == 2 * o)
        def _():
            mine[m, rows] = total[:, :128]

        @pl.when(y == 2 * o + 1)
        def _():
            mine[m, rows] = total[:, 128:]
        for t in range(2):
            for d in (1, 2, 3):
                @pl.when((y + d) % 4 == 2 * o + t)
                def _():
                    y_copy(m, i, r, t, d).start()

    def y_sent(m, i, r):
        for t in range(2):
            for d in (1, 2, 3):
                @pl.when((y + d) % 4 == 2 * (i // 3) + t)
                def _():
                    y_copy(m, i, r, t, d).wait_send()

    def y_all(m):
        for i, r in parts:
            if i in (0, 3):
                @pl.when(yh == i // 3)
                def _():
                    rows = rows_of(i, r)
                    total = mine[m, rows]
                    for d in (1, 2, 3):
                        net.arrived(ky[m, i // 3, r][d - 1], ry.at[m, d - 1, rows])
                        total += ry[m, d - 1, rows].astype(F32)
                    (lo, gt)[m][rows] = total.astype(BF)

    others = [((1 - yh) * 2 + c, ys[1]), ((1 - yh) * 2 + 1 - c, cross), (yh * 2 + 1 - c, mate)]
    gk = []

    def down_grad():
        need(("cx", 0), ("cx", 1), ("cm", 0), ("cm", 1))
        part = dot(H[...].reshape(1024, 512), C[...].reshape(1024, 1024), ((0,), (0,))).astype(BF)
        for g in range(4):
            gs[g] = part[:, g * 256:g * 256 + 256]
        gk.extend((net.push(gs.at[g], gr.at[gy], device), g) for g, device in others)
        gr[gy] = gs[gy]

    def down_done():
        for k, g in gk:
            net.arrived(k, gr.at[g])
        save(gr, gd_out)

    def down_share():
        dst = V.at[:, span(gy * 256, 256)]
        ks = [(net.push(wd.at[span(g * 512, 512)], dst, device), g) for g, device in others]

        def done():
            for k, g in ks:
                net.arrived(k, V.at[:, span(g * 256, 256)])
            v_load.wait()
        return done

    keep, ran = [], set()

    steps = [
        (ty, 0), (ty, 1), (cy,), (tx, 1, 0), (tx, 1, 1), (g1, 3, 0), (v,), (tx, 0, 1), (tm, 1),
        (g1, 3, 1), (tx, 0, 0), (g2, 3, 0), (cx, 0), (g1, 2, 0), (cx, 1), (g2, 3, 1), (g3, 3, 0),
        (g1, 0, 1), (tm, 0), (g2, 2, 0), (g3, 3, 1), (g1, 1, 0), (g2, 0, 1), (h1, 0, 0), (cm, 0),
        (g3, 2, 0), (g1, 0, 0), (g4, 3, 0), (h1, 1, 0), (g2, 1, 0), (h1, 0, 1), (g4, 2, 0),
        (g2, 0, 0), (g3, 0, 1), (h1, 3, 1), (g3, 1, 0), (g4, 3, 1), (cm, 1), (g5, 2, 0), (h2, 0, 0),
        (g3, 0, 0), (h1, 2, 0), (g5, 3, 0), (x1, 0, 3, 0), (g4, 0, 1), (h2, 0, 1), (h2, 1, 0),
        (g4, 0, 0), (g5, 3, 1), (x2, 0, 3, 0), (g4, 1, 0), (h2, 2, 0), (h2, 3, 1), (h3, 1, 0),
        (g5, 1, 0), (x3, 0, 3, 0), (g5, 0, 0), (x1, 0, 3, 1), (h3, 0, 0), (g5, 0, 1), (h1, 3, 0),
        (h3, 2, 0), (x1, 0, 0, 0), (x1, 0, 0, 1), (down_grad,), (h4, 1, 0), (x2, 0, 3, 1),
        (x2, 0, 0, 0), (h3, 0, 1), (h2, 3, 0), (h4, 0, 0), (h4, 2, 0), (h3, 3, 1), (h5, 1, 0),
        (x2, 0, 0, 1), (h4, 0, 1), (h5, 0, 0), (h3, 3, 0), (x1, 1, 0, 0), (h5, 2, 0), (h4, 3, 1),
        (h5, 0, 1), (x1, 1, 0, 1), (x3, 0, 0, 0), (h4, 3, 0), (x2, 1, 0, 0), (x3, 0, 3, 1),
        (h5, 3, 1), (x1, 1, 3, 1), (x3, 0, 0, 1), (x2, 1, 0, 1), (h5, 3, 0), (x1, 1, 3, 0),
        (x3, 1, 0, 0), (x2, 1, 3, 1), (x2, 1, 3, 0), (down_done,), (x3, 1, 0, 1), (x3, 1, 3, 1),
        (y_all, 0), (x3, 1, 3, 0), (y_all, 1),
    ]
    for f, *args in steps:
        f(*args)
        ran.add((f, *args))
        if f is tm and len([s for s in ran if s[0] is tm]) == 2:
            need(("tm", 0), ("tm", 1))
            save(T, t_out)
    for copy in keep:
        copy.wait()
    for m in range(2):
        for i, r in parts:
            if i in (0, 3):
                y_sent(m, i, r)
    net.drain()


def local(tok, cot, wg, wu, wd):
    any_, vmem = pl.BlockSpec(memory_space=pl.ANY), pl.BlockSpec(memory_space=pltpu.VMEM)
    S = jax.ShapeDtypeStruct
    scratch = [
        pltpu.VMEM((4, 256, 1024), BF),
        pltpu.VMEM((4, 256, 1024), BF),
        pltpu.VMEM((1024, 1024), BF),
        pltpu.VMEM((512, 1024), BF),
        pltpu.VMEM((4, 256, 512), BF),
        pltpu.VMEM((4, 256, 1024), BF),
        pltpu.VMEM((4, 256, 1024), F32),
        pltpu.VMEM((4, 256, 512), F32),
        pltpu.VMEM((4, 64, 1024), F32),
        pltpu.VMEM((4, 3, 64, 1024), BF),
        pltpu.VMEM((4, 2, 32, 1024), BF),
        pltpu.VMEM((4, 2, 64, 1024), BF),
        pltpu.VMEM((4, 3, 64, 512), BF),
        pltpu.VMEM((4, 2, 32, 512), BF),
        pltpu.VMEM((4, 2, 64, 512), BF),
        pltpu.VMEM((2, 2, 4, 256, 256), F32),
        pltpu.VMEM((2, 2, 4, 256, 256), F32),
        pltpu.VMEM((2, 2, 4, 256, 256), F32),
        pltpu.VMEM((2, 2, 3, 256, 256), XT),
        pltpu.VMEM((2, 2, 2, 128, 256), XT),
        pltpu.VMEM((2, 2, 2, 256, 256), XT),
        pltpu.VMEM((2, 2, 2, 256, 128), YT),
        pltpu.VMEM((2, 3, 256, 128), YT),
        pltpu.VMEM((2, 256, 128), F32),
        pltpu.VMEM((4, 512, 256), BF),
        pltpu.VMEM((4, 512, 256), BF),
        pltpu.SemaphoreType.DMA((NSEM,)),
        pltpu.SemaphoreType.DMA((NSEM,)),
    ]
    lo, gt, t_all, g_all, gd = pl.pallas_call(
        kernel,
        out_shape=[S((256, 128), BF), S((256, 128), BF), S((4, 256, 1024), BF),
                   S((4, 256, 1024), BF), S((4, 512, 256), BF)],
        in_specs=[any_] * 5,
        out_specs=[vmem, vmem, any_, any_, any_],
        scratch_shapes=scratch,
        compiler_params=pltpu.CompilerParams(
            collective_id=0, has_side_effects=True, vmem_limit_bytes=56 << 20),
        cost_estimate=pl.CostEstimate(flops=8_000_000_000, bytes_accessed=10_000_000, transcendentals=600_000),
        name="layer",
    )(tok, cot, wg, wu, wd)
    return weight_grads(lo, gt, t_all.reshape(1024, 1024), g_all.reshape(1024, 1024), gd.reshape(2048, 256))


def weight_grads_kernel(lo, gt, t_in, g_in, gd_in, lo_out, gt_out, gg_out, gu_out, gd_out, T, G, D, gg, gu, gd, sems):
    count = [0]

    def copy(src, dst):
        made = pltpu.make_async_copy(src, dst, sems.at[count[0]])
        count[0] += 1
        made.start()
        return made

    blocks = [pl.ds(n * 256, 256) for n in range(4)]
    first = [copy(g_in.at[rows], G.at[rows]) for rows in blocks]
    t_loads = [copy(t_in.at[:, cols], T.at[:, cols]) for cols in blocks]
    d_loads = [copy(gd_in.at[pl.ds(n * 1024, 1024)], D.at[pl.ds(n * 1024, 1024)]) for n in range(2)]
    small = [copy(lo, lo_out), copy(gt, gt_out)]
    for load in first:
        load.wait()
    stores = []
    for n in range(4):
        rows = blocks[n]
        t_loads[n].wait()
        part = dot(T[:, rows], G[...], ((0,), (0,)))
        gg[rows] = part[:, :512]
        stores.append(copy(gg.at[rows], gg_out.at[rows]))
        gu[rows] = part[:, 512:]
        stores.append(copy(gu.at[rows], gu_out.at[rows]))
        if n < 2:
            rows = pl.ds(n * 1024, 1024)
            d_loads[n].wait()
            gd[rows] = D[rows].astype(F32)
            stores.append(copy(gd.at[rows], gd_out.at[rows]))
    for made in stores + small:
        made.wait()


def weight_grads(lo, gt, t_all, g_all, gd):
    any_ = pl.BlockSpec(memory_space=pl.ANY)
    S = jax.ShapeDtypeStruct
    return pl.pallas_call(
        weight_grads_kernel,
        out_shape=[S((256, 128), BF), S((256, 128), BF), S((1024, 512), F32), S((1024, 512), F32),
                   S((2048, 256), F32)],
        in_specs=[any_] * 5,
        out_specs=[any_] * 5,
        scratch_shapes=[
            pltpu.VMEM((1024, 1024), BF), pltpu.VMEM((1024, 1024), BF), pltpu.VMEM((2048, 256), BF),
            pltpu.VMEM((1024, 512), F32), pltpu.VMEM((1024, 512), F32), pltpu.VMEM((2048, 256), F32),
            pltpu.SemaphoreType.DMA((24,))],
        compiler_params=pltpu.CompilerParams(vmem_limit_bytes=60 << 20),
        cost_estimate=pl.CostEstimate(flops=2_200_000_000, bytes_accessed=12_000_000, transcendentals=0),
        name="weight_grads",
    )(lo, gt, t_all, g_all, gd)


def solution(mesh):
    ins = (P("gy", ("gz", "gx")), P("gy", ("gz", "gx")), P("gz", ("gx", "gy")),
           P("gz", ("gx", "gy")), P("gx", ("gz", "gy")))
    outs = (P("gy", ("gz", "gx")), P("gy", ("gz", "gx")), P("gz", ("gx", "gy")),
            P("gz", ("gx", "gy")), P("gx", ("gz", "gy")))
    return jax.shard_map(local, mesh=mesh, in_specs=ins, out_specs=outs, check_vma=False)
```

```python
import jax
import jax.numpy as jnp
from jax import lax
from jax.experimental import pallas as pl
from jax.experimental.pallas import tpu as pltpu
from jax.sharding import PartitionSpec as P

MESH = pl.DeviceIdType.MESH
BF, F32 = jnp.bfloat16, jnp.float32
XT = jnp.bfloat16
YT = jnp.bfloat16
NSEM = 256
PARTS = (2, 1, 1, 2)
DIRECT_Z = (3,)
DIRECT_X = ((1, 3),)
TPARTS = 2


def dot(a, b, dims):
    return lax.dot_general(a, b, (dims, ((), ())), preferred_element_type=F32)


class Net:
    def __init__(self, send, recv):
        self.send, self.recv, self.used, self.out = send, recv, 0, []

    def slot(self):
        self.used += 1
        return self.used - 1

    def push(self, src, dst, device, k=None):
        k = self.slot() if k is None else k
        copy = pltpu.make_async_remote_copy(
            src_ref=src, dst_ref=dst, send_sem=self.send.at[k], recv_sem=self.recv.at[k],
            device_id=device, device_id_type=MESH)
        copy.start()
        self.out.append(copy)
        return k

    def local(self, src, dst):
        k = self.slot()
        copy = pltpu.make_async_copy(src, dst, self.recv.at[k])
        copy.start()
        return copy

    def arrived(self, k, landing):
        pltpu.make_async_copy(landing, landing, self.recv.at[k]).wait()

    def drain(self):
        for copy in self.out:
            copy.wait_send()
        self.out = []


class ReduceScatter:
    def __init__(self, net, part, sent, half, full, rows, pos, plus, minus):
        self.net, self.part, self.sent, self.half, self.full = net, part, sent, half, full
        self.rows, self.pos, self.plus, self.minus = rows, pos, plus, minus

    def start(self):
        m = self.rows // 2
        far = self.sent(0, 0, self.rows)
        far[...] = self.part((self.pos + 2) % 4, 0, self.rows)[...].astype(far.dtype)
        self.ka = self.net.push(self.sent(0, 0, m), self.half(0), self.plus)
        self.kb = self.net.push(self.sent(0, m, m), self.half(1), self.minus)

    def middle(self):
        m = self.rows // 2
        right, left = (self.pos + 1) % 4, (self.pos + 3) % 4
        net, part, sent, half = self.net, self.part, self.sent, self.half
        kind = half(0).dtype
        sent(1, m, m)[...] = part(right, m, m)[...].astype(kind)
        sent(2, 0, m)[...] = part(left, 0, m)[...].astype(kind)
        net.arrived(self.ka, half(0))
        sent(1, 0, m)[...] = (part(right, 0, m)[...] + half(0)[...].astype(F32)).astype(kind)
        self.kp = net.push(sent(1, 0, self.rows), self.full(0), self.plus)
        net.arrived(self.kb, half(1))
        sent(2, m, m)[...] = (part(left, m, m)[...] + half(1)[...].astype(F32)).astype(kind)
        self.km = net.push(sent(2, 0, self.rows), self.full(1), self.minus)

    def finish(self):
        self.net.arrived(self.kp, self.full(0))
        self.net.arrived(self.km, self.full(1))
        return (self.part(self.pos, 0, self.rows)[...] + self.full(0)[...].astype(F32)
                + self.full(1)[...].astype(F32))


class DirectScatter:
    def __init__(self, net, part, sent, full, rows, pos, devices):
        self.net, self.part, self.sent, self.full = net, part, sent, full
        self.rows, self.pos, self.devices = rows, pos, devices

    def start(self):
        self.ks = []
        for d in (1, 3, 2):
            out = self.sent(d - 1, 0, self.rows)
            out[...] = self.part((self.pos + d) % 4, 0, self.rows)[...].astype(out.dtype)
            self.ks.append((self.net.push(out, self.full(d - 1), self.devices[d - 1]), d - 1))

    def finish(self):
        total = self.part(self.pos, 0, self.rows)[...]
        for k, n in self.ks:
            self.net.arrived(k, self.full(n))
            total += self.full(n)[...].astype(F32)
        return total


class DirectGather:
    def __init__(self, net, slot, rows, pos, devices):
        self.net, self.slot, self.rows, self.pos, self.devices = net, slot, rows, pos, devices

    def start(self):
        own = self.slot(self.pos, 0, self.rows)
        self.ks = [(self.net.push(own, own, self.devices[d - 1]), d) for d in (1, 3, 2)]

    def finish(self):
        for k, d in self.ks:
            self.net.arrived(k, self.slot((self.pos + 4 - d) % 4, 0, self.rows))


class AllGather:
    def __init__(self, net, slot, rows, pos, plus, minus):
        self.net, self.slot, self.rows = net, slot, rows
        self.pos, self.plus, self.minus = pos, plus, minus

    def start(self):
        own = self.slot(self.pos, 0, self.rows)
        self.kp = self.net.push(own, own, self.plus)
        self.km = self.net.push(own, own, self.minus)

    def forward(self):
        m = self.rows // 2
        right, left = (self.pos + 1) % 4, (self.pos + 3) % 4
        self.net.arrived(self.kp, self.slot(left, 0, self.rows))
        first = self.slot(left, 0, m)
        self.ka = self.net.push(first, first, self.plus)
        self.net.arrived(self.km, self.slot(right, 0, self.rows))
        second = self.slot(right, m, m)
        self.kb = self.net.push(second, second, self.minus)

    def finish(self):
        m = self.rows // 2
        far = (self.pos + 2) % 4
        self.net.arrived(self.ka, self.slot(far, 0, m))
        self.net.arrived(self.kb, self.slot(far, m, m))


def kernel(tok, cot, wg, wu, wd, lo, gt, w_out, gd_out,
           T, C, W, V, H, G, PG, PH, GU, sg, hg, fg, sh, hh, fh,
           own, give, take, sx, hx, fx, sy, ry, mine, gs, gr, ww, send, recv):
    gx, gy, gz = lax.axis_index("gx"), lax.axis_index("gy"), lax.axis_index("gz")
    x, z, c = gx // 2, gz, gy % 2
    yh, yl = gy // 2, gx % 2
    y = yh * 2 + yl

    def at(x, y, z, c):
        return (x * 2 + y % 2, (y // 2) * 2 + c, z)

    def span(start, size):
        return pl.ds(pl.multiple_of(start, size), size)

    ys = [at(x, (y + d) % 4, z, c) for d in (1, 2, 3)]
    xs = [at((x + d) % 4, y, z, c) for d in (1, 2, 3)]
    zs = [at(x, y, (z + d) % 4, c) for d in (1, 2, 3)]
    zp, zm = zs[0], zs[2]
    mate = at(x, y, z, 1 - c)
    cross = at(x, (y + 2) % 4, z, 1 - c)
    net = Net(send, recv)

    loads = [net.local(tok, T.at[gy, :, span(gx * 128, 128)]),
             net.local(cot, C.at[gy, :, span(gx * 128, 128)])]
    w_loads = [net.local(wg, W.at[:, pl.ds(0, 512)]), net.local(wu, W.at[:, pl.ds(512, 512)])]
    v_load = net.local(wd.at[span(gy * 512, 512)], V.at[:, span(gy * 256, 256)])

    barrier = pltpu.get_barrier_semaphore()
    peers = ys + xs + zs + [mate, cross]
    for peer in peers:
        pl.semaphore_signal(barrier, inc=1, device_id=peer, device_id_type=MESH)
    pl.semaphore_wait(barrier, len(peers))

    waits = {}

    def need(*keys):
        for key in keys:
            if key in waits:
                waits.pop(key)()

    def gather_y(src, buf, r, n):
        rows = pl.ds(r * n, n)
        mine = buf.at[gy, rows, span(gx * 128, 128)]
        ks = [net.push(src.at[rows], mine, d) for d in ys]

        def done():
            for d, k in zip((3, 2, 1), ks):
                yy = (y + d) % 4
                net.arrived(k, buf.at[(yy // 2) * 2 + c, rows, span((x * 2 + yy % 2) * 128, 128)])
        return done

    def gather_x(buf, h, r, n):
        rows = pl.ds(r * n, n)
        mine = buf.at[h * 2 + c, rows, span(x * 256, 256)]
        ks = [net.push(mine, mine, d) for d in xs]

        def done():
            for d, k in zip((3, 2, 1), ks):
                net.arrived(k, buf.at[h * 2 + c, rows, span(((x + d) % 4) * 256, 256)])
        return done

    def share(buf, h):
        mine = buf.at[h * 2 + c]
        k = net.push(mine, mine, mate)
        return lambda: net.arrived(k, buf.at[h * 2 + 1 - c])

    chunk = [c, 1 - c, 2 + 1 - c, 2 + c]
    parts = [(i, r) for i in range(4) for r in range(PARTS[i])]
    rs_g, rs_h, ag_h, ag_g, rs_x = {}, {}, {}, {}, {}

    def ring_z(i, r, P, s, h, f):
        n = 256 // PARTS[i]
        q = n // 4
        return ReduceScatter(
            net, lambda k, a, m: P.at[i, span(r * n + k * q + a, m)],
            lambda k, a, m: s.at[i, k, pl.ds(r * q + a, m)],
            lambda k: h.at[i, k, pl.ds(r * q // 2, q // 2)],
            lambda k: f.at[i, k, pl.ds(r * q, q)], q, z, zp, zm)

    def gather_z(i, r, B):
        n = 256 // PARTS[i]
        q = n // 4

        def slot(k, a, m):
            return B.at[chunk[i], span(r * n + k * q + a, m)]
        if B is G and i in DIRECT_Z:
            return DirectGather(net, slot, q, z, zs)
        return AllGather(net, slot, q, z, zp, zm)

    def ring_x(m, o, r, n):
        if (m, 3 * o) in DIRECT_X:
            return DirectScatter(
                net, lambda k, a, l: own.at[m, o, k, pl.ds(r * n + a, l)],
                lambda k, a, l: sx.at[m, o, k, pl.ds(r * n + a, l)],
                lambda k: fx.at[m, o, k, pl.ds(r * n, n)], n, x, xs)
        return ReduceScatter(
            net, lambda k, a, l: own.at[m, o, k, pl.ds(r * n + a, l)],
            lambda k, a, l: sx.at[m, o, k, pl.ds(r * n + a, l)],
            lambda k: hx.at[m, o, k, pl.ds(r * n // 2, n // 2)],
            lambda k: fx.at[m, o, k, pl.ds(r * n, n)], n, x, xs[0], xs[2])

    for i, r in parts:
        rs_g[i, r] = ring_z(i, r, PG, sg, hg, fg)
        rs_h[i, r] = ring_z(i, r, PH, sh, hh, fh)
        ag_h[i, r] = gather_z(i, r, H)
        ag_g[i, r] = gather_z(i, r, G)
        if i in (0, 3):
            for m in range(2):
                rs_x[m, i // 3, r] = ring_x(m, i // 3, r, 256 // PARTS[i])

    def rows_of(i, r):
        n = 256 // PARTS[i]
        return pl.ds(r * n, n)

    def quarter(i, r):
        q = 64 // PARTS[i]
        return pl.ds(r * q, q)

    def all_of(copies):
        return lambda: [copy.wait() for copy in copies]

    waits["own"], waits["weights"] = all_of(loads), all_of(w_loads)

    def ty(r):
        waits["ty", r] = gather_y(tok, T, r, 256 // TPARTS)

    def tx(h, r):
        need("own", ("ty", r))
        waits["tx", h, r] = gather_x(T, h, r, 256 // TPARTS)

    def tm(h):
        need(*[("tx", h, r) for r in range(TPARTS)])
        waits["tm", h] = share(T, h)

    def cy():
        waits["cy"] = gather_y(cot, C, 0, 256)

    def cx(h):
        need("own", "cy")
        waits["cx", h] = gather_x(C, h, 0, 256)

    def cm(h):
        need(("cx", h))
        waits["cm", h] = share(C, h)

    def v():
        waits["v"] = down_share()

    def save(src, dst):
        keep.append(net.local(src, dst))

    def g1(i, r):
        need("weights")
        if i in (0, 3):
            need(*[("tx", i // 3, q) for q in ([r] if TPARTS == PARTS[i] else range(TPARTS))])
        else:
            need(("tm", i - 1))
        PG[i, rows_of(i, r)] = dot(T[chunk[i], rows_of(i, r)], W[...], ((1,), (0,)))
        rs_g[i, r].start()

    def g2(i, r):
        rs_g[i, r].middle()

    def g3(i, r):
        s = rs_g[i, r].finish()
        GU[i, quarter(i, r)] = s
        gate, up = s[:, :512], s[:, 512:]
        gather = ag_h[i, r]
        gather.slot(z, 0, gather.rows)[...] = (gate * jax.nn.sigmoid(gate) * up).astype(BF)
        gather.start()

    def g4(i, r):
        ag_h[i, r].forward()

    def h1(i, r):
        need("v", ("cx", i // 3) if i in (0, 3) else ("cm", i - 1))
        PH[i, rows_of(i, r)] = dot(C[chunk[i], rows_of(i, r)], V[...], ((1,), (1,)))
        rs_h[i, r].start()

    def h2(i, r):
        rs_h[i, r].middle()

    def h3(i, r):
        grad = rs_h[i, r].finish()
        gate, up = GU[i, quarter(i, r), :512], GU[i, quarter(i, r), 512:]
        s = jax.nn.sigmoid(gate)
        gather = ag_g[i, r]
        slot = gather.slot(z, 0, gather.rows)
        slot[:, :512] = (grad * up * s * (1.0 + gate * (1.0 - s))).astype(BF)
        slot[:, 512:] = (grad * (gate * s)).astype(BF)
        gather.start()

    def h4(i, r):
        ag_g[i, r].forward()

    took = {}

    def place(m, i, r, part):
        dst = (own.at[m, 0], give.at[m, 0], give.at[m, 1], own.at[m, 1])[i]
        rows = rows_of(i, r)
        for n in range(4):
            dst[n, rows] = part[:, n * 256:n * 256 + 256]
        if i in (1, 2):
            there = take.at[m, i - 1, :, rows]
            took[m, i - 1, r] = net.push(dst.at[:, rows], there, mate), there

    def g5(i, r):
        need("v")
        ag_h[i, r].finish()
        place(0, i, r, dot(H[chunk[i], rows_of(i, r)], V[...], ((1,), (0,))))

    def h5(i, r):
        ag_g[i, r].finish()
        place(1, i, r, dot(G[chunk[i], rows_of(i, r)], W[...], ((1,), (1,))))

    def weight_grad(q):
        cols = pl.ds(q * 256, 256)
        ww[q] = dot(T[:, :, cols].reshape(1024, 256), G[...].reshape(1024, 1024), ((0,), (0,))).astype(BF)
        save(ww.at[q], w_out.at[q])

    def x1(m, i, r):
        o = i // 3
        if PARTS[1 + o] == PARTS[i]:
            keys = [r]
        else:
            keys = range(PARTS[1 + o])
        for q in keys:
            if (m, o, q) in took:
                net.arrived(*took.pop((m, o, q)))
        rows = rows_of(i, r)
        for n in range(4):
            own[m, o, n, rows] += take[m, o, n, rows]
        rs_x[m, o, r].start()

    def x2(m, i, r):
        rs_x[m, i // 3, r].middle()

    ky = {(m, i // 3, r): [net.slot() for _ in range(3)] for m in range(2) for i, r in parts if i in (0, 3)}

    def y_copy(m, i, r, t, d):
        o, rows = i // 3, rows_of(i, r)
        k = ky[m, o, r][d - 1]
        return pltpu.make_async_remote_copy(
            src_ref=sy.at[m, o, t, rows], dst_ref=ry.at[m, d - 1, rows],
            send_sem=send.at[k], recv_sem=recv.at[k],
            device_id=at(x, 2 * o + t, z, c), device_id_type=MESH)

    def x3(m, i, r):
        o, rows = i // 3, rows_of(i, r)
        total = rs_x[m, o, r].finish()
        sy[m, o, 0, rows] = total[:, :128].astype(YT)
        sy[m, o, 1, rows] = total[:, 128:].astype(YT)

        @pl.when(y == 2 * o)
        def _():
            mine[m, rows] = total[:, :128]

        @pl.when(y == 2 * o + 1)
        def _():
            mine[m, rows] = total[:, 128:]
        for t in range(2):
            for d in (1, 2, 3):
                @pl.when((y + d) % 4 == 2 * o + t)
                def _():
                    y_copy(m, i, r, t, d).start()

    def y_sent(m, i, r):
        for t in range(2):
            for d in (1, 2, 3):
                @pl.when((y + d) % 4 == 2 * (i // 3) + t)
                def _():
                    y_copy(m, i, r, t, d).wait_send()

    def y_all(m):
        for i, r in parts:
            if i in (0, 3):
                @pl.when(yh == i // 3)
                def _():
                    rows = rows_of(i, r)
                    total = mine[m, rows]
                    for d in (1, 2, 3):
                        net.arrived(ky[m, i // 3, r][d - 1], ry.at[m, d - 1, rows])
                        total += ry[m, d - 1, rows].astype(F32)
                    (lo, gt)[m][rows] = total.astype(BF)

    others = [((1 - yh) * 2 + c, ys[1]), ((1 - yh) * 2 + 1 - c, cross), (yh * 2 + 1 - c, mate)]
    gk = []

    def down_grad():
        need(("cx", 0), ("cx", 1), ("cm", 0), ("cm", 1))
        part = dot(H[...].reshape(1024, 512), C[...].reshape(1024, 1024), ((0,), (0,))).astype(BF)
        for g in range(4):
            gs[g] = part[:, g * 256:g * 256 + 256]
        gk.extend((net.push(gs.at[g], gr.at[gy], device), g) for g, device in others)
        gr[gy] = gs[gy]

    def down_done():
        for k, g in gk:
            net.arrived(k, gr.at[g])
        save(gr, gd_out)

    def down_share():
        dst = V.at[:, span(gy * 256, 256)]
        ks = [(net.push(wd.at[span(g * 512, 512)], dst, device), g) for g, device in others]

        def done():
            for k, g in ks:
                net.arrived(k, V.at[:, span(g * 256, 256)])
            v_load.wait()
        return done

    keep = []

    steps = [
        (ty, 0), (ty, 1), (tx, 1, 0), (cy,), (v,), (tx, 1, 1), (g1, 3, 0), (tx, 0, 1), (tm, 1),
        (g1, 3, 1), (g2, 3, 0), (tx, 0, 0), (g1, 2, 0), (g1, 0, 1), (g2, 3, 1), (g3, 3, 0), (cx, 0),
        (g2, 2, 0), (g3, 3, 1), (tm, 0), (cx, 1), (g1, 0, 0), (g2, 0, 1), (g1, 1, 0), (g3, 2, 0),
        (g2, 0, 0), (g4, 3, 1), (g4, 3, 0), (cm, 0), (g2, 1, 0), (g3, 0, 0), (h1, 0, 1), (g3, 0, 1),
        (g5, 3, 1), (h1, 0, 0), (cm, 1), (h1, 1, 0), (g3, 1, 0), (g4, 2, 0), (h1, 2, 0), (g4, 0, 1),
        (g5, 3, 0), (h2, 0, 1), (h2, 1, 0), (g4, 1, 0), (g5, 2, 0), (h2, 0, 0), (g4, 0, 0),
        (h2, 2, 0), (g5, 0, 1), (h1, 3, 1), (h3, 1, 0), (g5, 1, 0), (h3, 0, 1), (g5, 0, 0),
        (h3, 0, 0), (x1, 0, 3, 0), (x1, 0, 0, 1), (down_grad,), (h4, 1, 0), (x1, 0, 3, 1),
        (x1, 0, 0, 0), (h3, 2, 0), (x2, 0, 3, 0), (h1, 3, 0), (h4, 0, 0), (x2, 0, 0, 1), (h2, 3, 1),
        (h4, 0, 1), (x2, 0, 3, 1), (x2, 0, 0, 0), (h5, 1, 0), (x3, 0, 3, 0), (h4, 2, 0),
        (x3, 0, 0, 1), (h2, 3, 0), (h5, 0, 0), (h3, 3, 1), (x1, 1, 0, 0), (h5, 0, 1), (x1, 1, 0, 1),
        (h5, 2, 0), (h3, 3, 0), (x2, 1, 0, 0), (x3, 0, 3, 1), (x3, 0, 0, 0), (x2, 1, 0, 1),
        (h5, 3, 1), (x1, 1, 3, 1), (down_done,), (x3, 1, 0, 0), (h5, 3, 0), (x1, 1, 3, 0),
        (weight_grad, 2), (x3, 1, 0, 1), (weight_grad, 3), (x3, 1, 3, 1), (x3, 1, 3, 0),
        (weight_grad, 0), (y_all, 0), (weight_grad, 1), (y_all, 1),
    ]
    for f, *args in steps:
        f(*args)
    for copy in keep:
        copy.wait()
    for m in range(2):
        for i, r in parts:
            if i in (0, 3):
                y_sent(m, i, r)
    net.drain()


def local(tok, cot, wg, wu, wd):
    any_, vmem = pl.BlockSpec(memory_space=pl.ANY), pl.BlockSpec(memory_space=pltpu.VMEM)
    S = jax.ShapeDtypeStruct
    scratch = [
        pltpu.VMEM((4, 256, 1024), BF),
        pltpu.VMEM((4, 256, 1024), BF),
        pltpu.VMEM((1024, 1024), BF),
        pltpu.VMEM((512, 1024), BF),
        pltpu.VMEM((4, 256, 512), BF),
        pltpu.VMEM((4, 256, 1024), BF),
        pltpu.VMEM((4, 256, 1024), F32),
        pltpu.VMEM((4, 256, 512), F32),
        pltpu.VMEM((4, 64, 1024), F32),
        pltpu.VMEM((4, 3, 64, 1024), BF),
        pltpu.VMEM((4, 2, 32, 1024), BF),
        pltpu.VMEM((4, 2, 64, 1024), BF),
        pltpu.VMEM((4, 3, 64, 512), BF),
        pltpu.VMEM((4, 2, 32, 512), BF),
        pltpu.VMEM((4, 2, 64, 512), BF),
        pltpu.VMEM((2, 2, 4, 256, 256), F32),
        pltpu.VMEM((2, 2, 4, 256, 256), F32),
        pltpu.VMEM((2, 2, 4, 256, 256), F32),
        pltpu.VMEM((2, 2, 3, 256, 256), XT),
        pltpu.VMEM((2, 2, 2, 128, 256), XT),
        pltpu.VMEM((2, 2, 3, 256, 256), XT),
        pltpu.VMEM((2, 2, 2, 256, 128), YT),
        pltpu.VMEM((2, 3, 256, 128), YT),
        pltpu.VMEM((2, 256, 128), F32),
        pltpu.VMEM((4, 512, 256), BF),
        pltpu.VMEM((4, 512, 256), BF),
        pltpu.VMEM((4, 256, 1024), BF),
        pltpu.SemaphoreType.DMA((NSEM,)),
        pltpu.SemaphoreType.DMA((NSEM,)),
    ]
    lo, gt, grads, gd = pl.pallas_call(
        kernel,
        out_shape=[S((256, 128), BF), S((256, 128), BF), S((4, 256, 1024), BF),
                   S((4, 512, 256), BF)],
        in_specs=[any_] * 5,
        out_specs=[vmem, vmem, any_, any_],
        scratch_shapes=scratch,
        compiler_params=pltpu.CompilerParams(
            collective_id=0, has_side_effects=True, vmem_limit_bytes=56 << 20),
        cost_estimate=pl.CostEstimate(flops=8_000_000_000, bytes_accessed=10_000_000, transcendentals=600_000),
        name="layer",
    )(tok, cot, wg, wu, wd)
    return widen(lo, gt, grads.reshape(1024, 1024), gd.reshape(2048, 256))


def widen_kernel(lo, gt, w_in, gd_in, lo_out, gt_out, gg_out, gu_out, gd_out, Wb, D, gg, gu, gd, sems):
    count = [0]

    def copy(src, dst):
        made = pltpu.make_async_copy(src, dst, sems.at[count[0]])
        count[0] += 1
        made.start()
        return made

    blocks = [(pl.ds(n * 256, 256), pl.ds(n * 512, 512)) for n in range(4)]
    loads = [(copy(w_in.at[a], Wb.at[a]), copy(gd_in.at[b], D.at[b])) for a, b in blocks]
    stores = [copy(lo, lo_out), copy(gt, gt_out)]
    for (a, b), (first, second) in zip(blocks, loads):
        first.wait()
        gg[a] = Wb[a, :512].astype(F32)
        stores.append(copy(gg.at[a], gg_out.at[a]))
        gu[a] = Wb[a, 512:].astype(F32)
        stores.append(copy(gu.at[a], gu_out.at[a]))
        second.wait()
        gd[b] = D[b].astype(F32)
        stores.append(copy(gd.at[b], gd_out.at[b]))
    for made in stores:
        made.wait()


def widen(lo, gt, grads, gd):
    any_ = pl.BlockSpec(memory_space=pl.ANY)
    S = jax.ShapeDtypeStruct
    return pl.pallas_call(
        widen_kernel,
        out_shape=[S((256, 128), BF), S((256, 128), BF), S((1024, 512), F32), S((1024, 512), F32),
                   S((2048, 256), F32)],
        in_specs=[any_] * 4,
        out_specs=[any_] * 5,
        scratch_shapes=[
            pltpu.VMEM((1024, 1024), BF), pltpu.VMEM((2048, 256), BF),
            pltpu.VMEM((1024, 512), F32), pltpu.VMEM((1024, 512), F32), pltpu.VMEM((2048, 256), F32),
            pltpu.SemaphoreType.DMA((24,))],
        compiler_params=pltpu.CompilerParams(vmem_limit_bytes=60 << 20),
        cost_estimate=pl.CostEstimate(flops=0, bytes_accessed=9_500_000, transcendentals=0),
        name="widen",
    )(lo, gt, grads, gd)


def solution(mesh):
    ins = (P("gy", ("gz", "gx")), P("gy", ("gz", "gx")), P("gz", ("gx", "gy")),
           P("gz", ("gx", "gy")), P("gx", ("gz", "gy")))
    outs = (P("gy", ("gz", "gx")), P("gy", ("gz", "gx")), P("gz", ("gx", "gy")),
            P("gz", ("gx", "gy")), P("gx", ("gz", "gy")))
    return jax.shard_map(local, mesh=mesh, in_specs=ins, out_specs=outs, check_vma=False)
```

```python
import jax
import jax.numpy as jnp
from jax import lax
from jax.experimental import pallas as pl
from jax.experimental.pallas import tpu as pltpu
from jax.sharding import PartitionSpec as P

MESH = pl.DeviceIdType.MESH
BF, F32 = jnp.bfloat16, jnp.float32
XT = jnp.bfloat16
YT = jnp.bfloat16
NSEM = 256
PARTS = (2, 1, 1, 2)
DIRECT_Z = (3,)
DIRECT_X = ((1, 3),)
TPARTS = 2


def dot(a, b, dims):
    return lax.dot_general(a, b, (dims, ((), ())), preferred_element_type=F32)


class Net:
    def __init__(self, send, recv):
        self.send, self.recv, self.used, self.out = send, recv, 0, []

    def slot(self):
        self.used += 1
        return self.used - 1

    def push(self, src, dst, device, k=None):
        k = self.slot() if k is None else k
        copy = pltpu.make_async_remote_copy(
            src_ref=src, dst_ref=dst, send_sem=self.send.at[k], recv_sem=self.recv.at[k],
            device_id=device, device_id_type=MESH)
        copy.start()
        self.out.append(copy)
        return k

    def local(self, src, dst):
        k = self.slot()
        copy = pltpu.make_async_copy(src, dst, self.recv.at[k])
        copy.start()
        return copy

    def arrived(self, k, landing):
        pltpu.make_async_copy(landing, landing, self.recv.at[k]).wait()

    def drain(self):
        for copy in self.out:
            copy.wait_send()
        self.out = []


class ReduceScatter:
    def __init__(self, net, part, sent, half, full, rows, pos, plus, minus):
        self.net, self.part, self.sent, self.half, self.full = net, part, sent, half, full
        self.rows, self.pos, self.plus, self.minus = rows, pos, plus, minus

    def start(self):
        m = self.rows // 2
        far = self.sent(0, 0, self.rows)
        far[...] = self.part((self.pos + 2) % 4, 0, self.rows)[...].astype(far.dtype)
        self.ka = self.net.push(self.sent(0, 0, m), self.half(0), self.plus)
        self.kb = self.net.push(self.sent(0, m, m), self.half(1), self.minus)

    def middle(self):
        m = self.rows // 2
        right, left = (self.pos + 1) % 4, (self.pos + 3) % 4
        net, part, sent, half = self.net, self.part, self.sent, self.half
        kind = half(0).dtype
        sent(1, m, m)[...] = part(right, m, m)[...].astype(kind)
        sent(2, 0, m)[...] = part(left, 0, m)[...].astype(kind)
        net.arrived(self.ka, half(0))
        sent(1, 0, m)[...] = (part(right, 0, m)[...] + half(0)[...].astype(F32)).astype(kind)
        self.kp = net.push(sent(1, 0, self.rows), self.full(0), self.plus)
        net.arrived(self.kb, half(1))
        sent(2, m, m)[...] = (part(left, m, m)[...] + half(1)[...].astype(F32)).astype(kind)
        self.km = net.push(sent(2, 0, self.rows), self.full(1), self.minus)

    def finish(self):
        self.net.arrived(self.kp, self.full(0))
        self.net.arrived(self.km, self.full(1))
        return (self.part(self.pos, 0, self.rows)[...] + self.full(0)[...].astype(F32)
                + self.full(1)[...].astype(F32))


class DirectScatter:
    def __init__(self, net, part, sent, full, rows, pos, devices):
        self.net, self.part, self.sent, self.full = net, part, sent, full
        self.rows, self.pos, self.devices = rows, pos, devices

    def start(self):
        self.ks = []
        for d in (1, 3, 2):
            out = self.sent(d - 1, 0, self.rows)
            out[...] = self.part((self.pos + d) % 4, 0, self.rows)[...].astype(out.dtype)
            self.ks.append((self.net.push(out, self.full(d - 1), self.devices[d - 1]), d - 1))

    def finish(self):
        total = self.part(self.pos, 0, self.rows)[...]
        for k, n in self.ks:
            self.net.arrived(k, self.full(n))
            total += self.full(n)[...].astype(F32)
        return total


class DirectGather:
    def __init__(self, net, slot, rows, pos, devices):
        self.net, self.slot, self.rows, self.pos, self.devices = net, slot, rows, pos, devices

    def start(self):
        own = self.slot(self.pos, 0, self.rows)
        self.ks = [(self.net.push(own, own, self.devices[d - 1]), d) for d in (1, 3, 2)]

    def finish(self):
        for k, d in self.ks:
            self.net.arrived(k, self.slot((self.pos + 4 - d) % 4, 0, self.rows))


class AllGather:
    def __init__(self, net, slot, rows, pos, plus, minus):
        self.net, self.slot, self.rows = net, slot, rows
        self.pos, self.plus, self.minus = pos, plus, minus

    def start(self):
        own = self.slot(self.pos, 0, self.rows)
        self.kp = self.net.push(own, own, self.plus)
        self.km = self.net.push(own, own, self.minus)

    def forward(self):
        m = self.rows // 2
        right, left = (self.pos + 1) % 4, (self.pos + 3) % 4
        self.net.arrived(self.kp, self.slot(left, 0, self.rows))
        first = self.slot(left, 0, m)
        self.ka = self.net.push(first, first, self.plus)
        self.net.arrived(self.km, self.slot(right, 0, self.rows))
        second = self.slot(right, m, m)
        self.kb = self.net.push(second, second, self.minus)

    def finish(self):
        m = self.rows // 2
        far = (self.pos + 2) % 4
        self.net.arrived(self.ka, self.slot(far, 0, m))
        self.net.arrived(self.kb, self.slot(far, m, m))


def kernel(tok, cot, wg, wu, wd, lo, gt, w_out, gd_out,
           T, C, W, V, H, G, PG, PH, GU, sg, hg, fg, sh, hh, fh,
           own, give, take, sx, hx, fx, sy, ry, mine, gs, gr, ww, send, recv):
    gx, gy, gz = lax.axis_index("gx"), lax.axis_index("gy"), lax.axis_index("gz")
    x, z, c = gx // 2, gz, gy % 2
    yh, yl = gy // 2, gx % 2
    y = yh * 2 + yl

    def at(x, y, z, c):
        return (x * 2 + y % 2, (y // 2) * 2 + c, z)

    def span(start, size):
        return pl.ds(pl.multiple_of(start, size), size)

    ys = [at(x, (y + d) % 4, z, c) for d in (1, 2, 3)]
    xs = [at((x + d) % 4, y, z, c) for d in (1, 2, 3)]
    zs = [at(x, y, (z + d) % 4, c) for d in (1, 2, 3)]
    zp, zm = zs[0], zs[2]
    mate = at(x, y, z, 1 - c)
    cross = at(x, (y + 2) % 4, z, 1 - c)
    net = Net(send, recv)

    loads = [net.local(tok, T.at[gy, :, span(gx * 128, 128)]),
             net.local(cot, C.at[gy, :, span(gx * 128, 128)])]
    w_loads = [net.local(wg, W.at[:, pl.ds(0, 512)]), net.local(wu, W.at[:, pl.ds(512, 512)])]
    v_load = net.local(wd.at[span(gy * 512, 512)], V.at[:, span(gy * 256, 256)])

    barrier = pltpu.get_barrier_semaphore()
    peers = ys + xs + zs + [mate, cross]
    for peer in peers:
        pl.semaphore_signal(barrier, inc=1, device_id=peer, device_id_type=MESH)
    pl.semaphore_wait(barrier, len(peers))

    waits = {}

    def need(*keys):
        for key in keys:
            if key in waits:
                waits.pop(key)()

    def gather_y(src, buf, r, n):
        rows = pl.ds(r * n, n)
        mine = buf.at[gy, rows, span(gx * 128, 128)]
        ks = [net.push(src.at[rows], mine, d) for d in ys]

        def done():
            for d, k in zip((3, 2, 1), ks):
                yy = (y + d) % 4
                net.arrived(k, buf.at[(yy // 2) * 2 + c, rows, span((x * 2 + yy % 2) * 128, 128)])
        return done

    def gather_x(buf, h, r, n):
        rows = pl.ds(r * n, n)
        mine = buf.at[h * 2 + c, rows, span(x * 256, 256)]
        ks = [net.push(mine, mine, d) for d in xs]

        def done():
            for d, k in zip((3, 2, 1), ks):
                net.arrived(k, buf.at[h * 2 + c, rows, span(((x + d) % 4) * 256, 256)])
        return done

    def share(buf, h):
        mine = buf.at[h * 2 + c]
        k = net.push(mine, mine, mate)
        return lambda: net.arrived(k, buf.at[h * 2 + 1 - c])

    chunk = [c, 1 - c, 2 + 1 - c, 2 + c]
    parts = [(i, r) for i in range(4) for r in range(PARTS[i])]
    rs_g, rs_h, ag_h, ag_g, rs_x = {}, {}, {}, {}, {}

    def ring_z(i, r, P, s, h, f):
        n = 256 // PARTS[i]
        q = n // 4
        return ReduceScatter(
            net, lambda k, a, m: P.at[i, span(r * n + k * q + a, m)],
            lambda k, a, m: s.at[i, k, pl.ds(r * q + a, m)],
            lambda k: h.at[i, k, pl.ds(r * q // 2, q // 2)],
            lambda k: f.at[i, k, pl.ds(r * q, q)], q, z, zp, zm)

    def gather_z(i, r, B):
        n = 256 // PARTS[i]
        q = n // 4

        def slot(k, a, m):
            return B.at[chunk[i], span(r * n + k * q + a, m)]
        if B is G and i in DIRECT_Z:
            return DirectGather(net, slot, q, z, zs)
        return AllGather(net, slot, q, z, zp, zm)

    def ring_x(m, o, r, n):
        if (m, 3 * o) in DIRECT_X:
            return DirectScatter(
                net, lambda k, a, l: own.at[m, o, k, pl.ds(r * n + a, l)],
                lambda k, a, l: sx.at[m, o, k, pl.ds(r * n + a, l)],
                lambda k: fx.at[m, o, k, pl.ds(r * n, n)], n, x, xs)
        return ReduceScatter(
            net, lambda k, a, l: own.at[m, o, k, pl.ds(r * n + a, l)],
            lambda k, a, l: sx.at[m, o, k, pl.ds(r * n + a, l)],
            lambda k: hx.at[m, o, k, pl.ds(r * n // 2, n // 2)],
            lambda k: fx.at[m, o, k, pl.ds(r * n, n)], n, x, xs[0], xs[2])

    for i, r in parts:
        rs_g[i, r] = ring_z(i, r, PG, sg, hg, fg)
        rs_h[i, r] = ring_z(i, r, PH, sh, hh, fh)
        ag_h[i, r] = gather_z(i, r, H)
        ag_g[i, r] = gather_z(i, r, G)
        if i in (0, 3):
            for m in range(2):
                rs_x[m, i // 3, r] = ring_x(m, i // 3, r, 256 // PARTS[i])

    def rows_of(i, r):
        n = 256 // PARTS[i]
        return pl.ds(r * n, n)

    def quarter(i, r):
        q = 64 // PARTS[i]
        return pl.ds(r * q, q)

    def all_of(copies):
        return lambda: [copy.wait() for copy in copies]

    waits["own"], waits["weights"] = all_of(loads), all_of(w_loads)

    def ty(r):
        waits["ty", r] = gather_y(tok, T, r, 256 // TPARTS)

    def tx(h, r):
        need("own", ("ty", r))
        waits["tx", h, r] = gather_x(T, h, r, 256 // TPARTS)

    def tm(h):
        need(*[("tx", h, r) for r in range(TPARTS)])
        waits["tm", h] = share(T, h)

    def cy():
        waits["cy"] = gather_y(cot, C, 0, 256)

    def cx(h):
        need("own", "cy")
        waits["cx", h] = gather_x(C, h, 0, 256)

    def cm(h):
        need(("cx", h))
        waits["cm", h] = share(C, h)

    def v():
        waits["v"] = down_share()

    def save(src, dst):
        keep.append(net.local(src, dst))

    def g1(i, r):
        need("weights")
        if i in (0, 3):
            need(*[("tx", i // 3, q) for q in ([r] if TPARTS == PARTS[i] else range(TPARTS))])
        else:
            need(("tm", i - 1))
        PG[i, rows_of(i, r)] = dot(T[chunk[i], rows_of(i, r)], W[...], ((1,), (0,)))
        rs_g[i, r].start()

    def g2(i, r):
        rs_g[i, r].middle()

    def g3(i, r):
        s = rs_g[i, r].finish()
        GU[i, quarter(i, r)] = s
        gate, up = s[:, :512], s[:, 512:]
        gather = ag_h[i, r]
        gather.slot(z, 0, gather.rows)[...] = (gate * jax.nn.sigmoid(gate) * up).astype(BF)
        gather.start()

    def g4(i, r):
        ag_h[i, r].forward()

    def h1(i, r):
        need("v", ("cx", i // 3) if i in (0, 3) else ("cm", i - 1))
        PH[i, rows_of(i, r)] = dot(C[chunk[i], rows_of(i, r)], V[...], ((1,), (1,)))
        rs_h[i, r].start()

    def h2(i, r):
        rs_h[i, r].middle()

    def h3(i, r):
        grad = rs_h[i, r].finish()
        gate, up = GU[i, quarter(i, r), :512], GU[i, quarter(i, r), 512:]
        s = jax.nn.sigmoid(gate)
        gather = ag_g[i, r]
        slot = gather.slot(z, 0, gather.rows)
        slot[:, :512] = (grad * up * s * (1.0 + gate * (1.0 - s))).astype(BF)
        slot[:, 512:] = (grad * (gate * s)).astype(BF)
        gather.start()

    def h4(i, r):
        ag_g[i, r].forward()

    took = {}

    def place(m, i, r, part):
        dst = (own.at[m, 0], give.at[m, 0], give.at[m, 1], own.at[m, 1])[i]
        rows = rows_of(i, r)
        for n in range(4):
            dst[n, rows] = part[:, n * 256:n * 256 + 256]
        if i in (1, 2):
            there = take.at[m, i - 1, :, rows]
            took[m, i - 1, r] = net.push(dst.at[:, rows], there, mate), there

    def g5(i, r):
        need("v")
        ag_h[i, r].finish()
        place(0, i, r, dot(H[chunk[i], rows_of(i, r)], V[...], ((1,), (0,))))

    def h5(i, r):
        ag_g[i, r].finish()
        place(1, i, r, dot(G[chunk[i], rows_of(i, r)], W[...], ((1,), (1,))))

    def weight_grad(q):
        cols = pl.ds(q * 256, 256)
        ww[q] = dot(T[:, :, cols].reshape(1024, 256), G[...].reshape(1024, 1024), ((0,), (0,))).astype(BF)
        save(ww.at[q], w_out.at[q])

    def x1(m, i, r):
        o = i // 3
        if PARTS[1 + o] == PARTS[i]:
            keys = [r]
        else:
            keys = range(PARTS[1 + o])
        for q in keys:
            if (m, o, q) in took:
                net.arrived(*took.pop((m, o, q)))
        rows = rows_of(i, r)
        for n in range(4):
            own[m, o, n, rows] += take[m, o, n, rows]
        rs_x[m, o, r].start()

    def x2(m, i, r):
        rs_x[m, i // 3, r].middle()

    ky = {(m, i // 3, r): [net.slot() for _ in range(3)] for m in range(2) for i, r in parts if i in (0, 3)}

    def y_copy(m, i, r, t, d):
        o, rows = i // 3, rows_of(i, r)
        k = ky[m, o, r][d - 1]
        return pltpu.make_async_remote_copy(
            src_ref=sy.at[m, o, t, rows], dst_ref=ry.at[m, d - 1, rows],
            send_sem=send.at[k], recv_sem=recv.at[k],
            device_id=at(x, 2 * o + t, z, c), device_id_type=MESH)

    def x3(m, i, r):
        o, rows = i // 3, rows_of(i, r)
        total = rs_x[m, o, r].finish()
        sy[m, o, 0, rows] = total[:, :128].astype(YT)
        sy[m, o, 1, rows] = total[:, 128:].astype(YT)

        @pl.when(y == 2 * o)
        def _():
            mine[m, rows] = total[:, :128]

        @pl.when(y == 2 * o + 1)
        def _():
            mine[m, rows] = total[:, 128:]
        for t in range(2):
            for d in (1, 2, 3):
                @pl.when((y + d) % 4 == 2 * o + t)
                def _():
                    y_copy(m, i, r, t, d).start()

    def y_sent(m, i, r):
        for t in range(2):
            for d in (1, 2, 3):
                @pl.when((y + d) % 4 == 2 * (i // 3) + t)
                def _():
                    y_copy(m, i, r, t, d).wait_send()

    def y_all(m):
        for i, r in parts:
            if i in (0, 3):
                @pl.when(yh == i // 3)
                def _():
                    rows = rows_of(i, r)
                    total = mine[m, rows]
                    for d in (1, 2, 3):
                        net.arrived(ky[m, i // 3, r][d - 1], ry.at[m, d - 1, rows])
                        total += ry[m, d - 1, rows].astype(F32)
                    (lo, gt)[m][rows] = total.astype(BF)

    others = [((1 - yh) * 2 + c, ys[1]), ((1 - yh) * 2 + 1 - c, cross), (yh * 2 + 1 - c, mate)]
    gk = []

    def down_grad():
        need(("cx", 0), ("cx", 1), ("cm", 0), ("cm", 1))
        part = dot(H[...].reshape(1024, 512), C[...].reshape(1024, 1024), ((0,), (0,))).astype(BF)
        for g in range(4):
            gs[g] = part[:, g * 256:g * 256 + 256]
        gk.extend((net.push(gs.at[g], gr.at[gy], device), g) for g, device in others)
        gr[gy] = gs[gy]

    def down_done():
        for k, g in gk:
            net.arrived(k, gr.at[g])
        save(gr, gd_out)

    def down_share():
        dst = V.at[:, span(gy * 256, 256)]
        ks = [(net.push(wd.at[span(g * 512, 512)], dst, device), g) for g, device in others]

        def done():
            for k, g in ks:
                net.arrived(k, V.at[:, span(g * 256, 256)])
            v_load.wait()
        return done

    keep = []

    steps = [
        (ty, 0), (ty, 1), (tx, 1, 0), (cy,), (v,), (tx, 1, 1), (g1, 3, 0), (tx, 0, 1), (tm, 1),
        (g1, 3, 1), (g2, 3, 0), (tx, 0, 0), (g1, 2, 0), (g1, 0, 1), (g2, 3, 1), (g3, 3, 0), (cx, 0),
        (g2, 2, 0), (g3, 3, 1), (tm, 0), (cx, 1), (g1, 0, 0), (g2, 0, 1), (g1, 1, 0), (g3, 2, 0),
        (g2, 0, 0), (g4, 3, 1), (g4, 3, 0), (cm, 0), (g2, 1, 0), (g3, 0, 0), (h1, 0, 1), (g3, 0, 1),
        (g5, 3, 1), (h1, 0, 0), (cm, 1), (h1, 1, 0), (g3, 1, 0), (g4, 2, 0), (h1, 2, 0), (g4, 0, 1),
        (g5, 3, 0), (h2, 0, 1), (h2, 1, 0), (g4, 1, 0), (g5, 2, 0), (h2, 0, 0), (g4, 0, 0),
        (h2, 2, 0), (g5, 0, 1), (h1, 3, 1), (h3, 1, 0), (g5, 1, 0), (h3, 0, 1), (g5, 0, 0),
        (h3, 0, 0), (x1, 0, 3, 0), (x1, 0, 0, 1), (down_grad,), (h4, 1, 0), (x1, 0, 3, 1),
        (x1, 0, 0, 0), (h3, 2, 0), (x2, 0, 3, 0), (h1, 3, 0), (h4, 0, 0), (x2, 0, 0, 1), (h2, 3, 1),
        (h4, 0, 1), (x2, 0, 3, 1), (x2, 0, 0, 0), (h5, 1, 0), (x3, 0, 3, 0), (h4, 2, 0),
        (x3, 0, 0, 1), (h2, 3, 0), (h5, 0, 0), (h3, 3, 1), (x1, 1, 0, 0), (h5, 0, 1), (x1, 1, 0, 1),
        (h5, 2, 0), (h3, 3, 0), (x2, 1, 0, 0), (x3, 0, 3, 1), (x3, 0, 0, 0), (x2, 1, 0, 1),
        (h5, 3, 1), (x1, 1, 3, 1), (down_done,), (x3, 1, 0, 0), (h5, 3, 0), (x1, 1, 3, 0),
        (weight_grad, 2), (x3, 1, 0, 1), (weight_grad, 3), (x3, 1, 3, 1), (x3, 1, 3, 0),
        (weight_grad, 0), (y_all, 0), (weight_grad, 1), (y_all, 1),
    ]
    for f, *args in steps:
        f(*args)
    for copy in keep:
        copy.wait()
    for m in range(2):
        for i, r in parts:
            if i in (0, 3):
                y_sent(m, i, r)
    net.drain()


def local(tok, cot, wg, wu, wd):
    any_, vmem = pl.BlockSpec(memory_space=pl.ANY), pl.BlockSpec(memory_space=pltpu.VMEM)
    S = jax.ShapeDtypeStruct
    scratch = [
        pltpu.VMEM((4, 256, 1024), BF),
        pltpu.VMEM((4, 256, 1024), BF),
        pltpu.VMEM((1024, 1024), BF),
        pltpu.VMEM((512, 1024), BF),
        pltpu.VMEM((4, 256, 512), BF),
        pltpu.VMEM((4, 256, 1024), BF),
        pltpu.VMEM((4, 256, 1024), F32),
        pltpu.VMEM((4, 256, 512), F32),
        pltpu.VMEM((4, 64, 1024), F32),
        pltpu.VMEM((4, 3, 64, 1024), BF),
        pltpu.VMEM((4, 2, 32, 1024), BF),
        pltpu.VMEM((4, 2, 64, 1024), BF),
        pltpu.VMEM((4, 3, 64, 512), BF),
        pltpu.VMEM((4, 2, 32, 512), BF),
        pltpu.VMEM((4, 2, 64, 512), BF),
        pltpu.VMEM((2, 2, 4, 256, 256), F32),
        pltpu.VMEM((2, 2, 4, 256, 256), F32),
        pltpu.VMEM((2, 2, 4, 256, 256), F32),
        pltpu.VMEM((2, 2, 3, 256, 256), XT),
        pltpu.VMEM((2, 2, 2, 128, 256), XT),
        pltpu.VMEM((2, 2, 3, 256, 256), XT),
        pltpu.VMEM((2, 2, 2, 256, 128), YT),
        pltpu.VMEM((2, 3, 256, 128), YT),
        pltpu.VMEM((2, 256, 128), F32),
        pltpu.VMEM((4, 512, 256), BF),
        pltpu.VMEM((4, 512, 256), BF),
        pltpu.VMEM((4, 256, 1024), BF),
        pltpu.SemaphoreType.DMA((NSEM,)),
        pltpu.SemaphoreType.DMA((NSEM,)),
    ]
    lo, gt, grads, gd = pl.pallas_call(
        kernel,
        out_shape=[S((256, 128), BF), S((256, 128), BF), S((4, 256, 1024), BF),
                   S((4, 512, 256), BF)],
        in_specs=[any_] * 5,
        out_specs=[vmem, vmem, any_, any_],
        scratch_shapes=scratch,
        compiler_params=pltpu.CompilerParams(
            collective_id=0, has_side_effects=True, vmem_limit_bytes=56 << 20),
        cost_estimate=pl.CostEstimate(flops=8_000_000_000, bytes_accessed=10_000_000, transcendentals=600_000),
        name="layer",
    )(tok, cot, wg, wu, wd)
    return widen(lo, gt, grads.reshape(1024, 1024), gd.reshape(2048, 256))


def widen_kernel(lo, gt, w_in, gd_in, lo_out, gt_out, gg_out, gu_out, gd_out, Wb, D, gg, gu, gd, small_buf, sems):
    count = [0]

    def copy(src, dst):
        made = pltpu.make_async_copy(src, dst, sems.at[count[0]])
        count[0] += 1
        made.start()
        return made

    blocks = [(pl.ds(n * 128, 128), pl.ds(n * 256, 256)) for n in range(8)]
    loads = [(copy(w_in.at[a], Wb.at[a]), copy(gd_in.at[b], D.at[b])) for a, b in blocks]
    small = [copy(lo, small_buf.at[0]), copy(gt, small_buf.at[1])]
    stores = []
    for (a, b), (first, second) in zip(blocks, loads):
        first.wait()
        gg[a] = Wb[a, :512].astype(F32)
        stores.append(copy(gg.at[a], gg_out.at[a]))
        gu[a] = Wb[a, 512:].astype(F32)
        stores.append(copy(gu.at[a], gu_out.at[a]))
        second.wait()
        gd[b] = D[b].astype(F32)
        stores.append(copy(gd.at[b], gd_out.at[b]))
        if small:
            for made in small:
                made.wait()
            stores += [copy(small_buf.at[0], lo_out), copy(small_buf.at[1], gt_out)]
            small = []
    for made in stores:
        made.wait()


def widen(lo, gt, grads, gd):
    any_ = pl.BlockSpec(memory_space=pl.ANY)
    S = jax.ShapeDtypeStruct
    return pl.pallas_call(
        widen_kernel,
        out_shape=[S((256, 128), BF), S((256, 128), BF), S((1024, 512), F32), S((1024, 512), F32),
                   S((2048, 256), F32)],
        in_specs=[any_] * 4,
        out_specs=[any_] * 5,
        scratch_shapes=[
            pltpu.VMEM((1024, 1024), BF), pltpu.VMEM((2048, 256), BF),
            pltpu.VMEM((1024, 512), F32), pltpu.VMEM((1024, 512), F32), pltpu.VMEM((2048, 256), F32),
            pltpu.VMEM((2, 256, 128), BF), pltpu.SemaphoreType.DMA((48,))],
        compiler_params=pltpu.CompilerParams(vmem_limit_bytes=60 << 20),
        cost_estimate=pl.CostEstimate(flops=0, bytes_accessed=9_500_000, transcendentals=0),
        name="widen",
    )(lo, gt, grads, gd)


def solution(mesh):
    ins = (P("gy", ("gz", "gx")), P("gy", ("gz", "gx")), P("gz", ("gx", "gy")),
           P("gz", ("gx", "gy")), P("gx", ("gz", "gy")))
    outs = (P("gy", ("gz", "gx")), P("gy", ("gz", "gx")), P("gz", ("gx", "gy")),
            P("gz", ("gx", "gy")), P("gx", ("gz", "gy")))
    return jax.shard_map(local, mesh=mesh, in_specs=ins, out_specs=outs, check_vma=False)
```
